32 devices in a mesh: dp: 2 (over x), expert: 16 (over z, y, core).
Axes of the slice: x: 2, y: 2, z: 4, core: 2. Of those that a mesh axis runs over, the one named last changes fastest.
Arguments:
- tokens: bfloat16 [4096, 4096], P(('dp', 'expert')), may hold values from -6 to 6
- routes: int32 [32, 2, 4], P(('dp', 'expert')), may hold values from 0 to 127, as said below
- gate_values: float32 [32, 2, 4], P(('dp', 'expert')), may hold values from 0.1 to 1
- gate_weight: bfloat16 [16, 4096, 256], P('expert', 'dp'), may hold values from -0.09375 to 0.09375
- up_weight: bfloat16 [16, 4096, 256], P('expert', 'dp'), may hold values from -0.09375 to 0.09375
- down_weight: bfloat16 [16, 4096, 256], P('expert', 'dp'), may hold values from -0.125 to 0.125
- cotangent: bfloat16 [4096, 4096], P(('dp', 'expert')), may hold values from -6 to 6
Outputs:
- layer_out: bfloat16 [4096, 4096], P(('dp', 'expert'))
- token_grad: bfloat16 [4096, 4096], P(('dp', 'expert'))
- gate_grad: bfloat16 [16, 4096, 256], P('expert', 'dp')
- up_grad: bfloat16 [16, 4096, 256], P('expert', 'dp')
- down_grad: bfloat16 [16, 4096, 256], P('expert', 'dp')
The draws below stay inside these ranges and needn't reach their ends.
Inputs may be any that keep to these rules, and one draw needn't show every extreme that they name: `routes`: for each home block and each expert, 4 distinct positions within that block.
All inputs are finite; a program needn't handle non-finite values.
Results may differ from the reference program's by a relative error of at most 0.025.
Values may be sent and summed in bfloat16 or wider, within the bound.
No kernel may reach another device: no remote copies, remote signals or barrier semaphores. Data moves between devices by JAX's collectives and lax.ppermute only.
A program may use at most 128 MiB of HBM per device.

```python
import math
import jax
import jax.numpy as jnp

D = 4096
FF = 2048
SPLIT = 8
TOK_DEV = 128
HID_DEV = 256
EXPERTS = 2
SLOT = 4
HOMES = 32
TOKENS = 4096
N_DP = 2
N_EXPERT = 16


def draw_routes(key, part):
    subkeys = jax.random.split(key, HOMES * EXPERTS)

    def pick_positions(subkey):
        return jax.random.permutation(subkey, TOK_DEV)[:SLOT]
    chosen = jax.vmap(pick_positions)(subkeys)
    return chosen.reshape(HOMES, EXPERTS, SLOT).astype(jnp.int32)


def block_levels(stream_key, dims, cuts, smallest, top_value):
    def one(axis_at, shards_of):
        steps = jax.random.uniform(jax.random.fold_in(jax.random.fold_in(stream_key, 6), axis_at), (shards_of,), jnp.float32, smallest / len(cuts), top_value / len(cuts))
        return jnp.repeat(jnp.exp(steps), dims[axis_at] // shards_of).reshape((-1,) + (1,) * (len(dims) - axis_at - 1))

    level = one(*cuts[0])
    for cut in cuts[1:]:
        level = level * one(*cut)
    return level


def bell_draw(key, extent, width, most, cuts=(), kind=jnp.bfloat16):
    entries = jax.random.normal(key, extent, jnp.float32) * width
    if len(cuts) > 0:
        entries = block_levels(key, extent, cuts, -0.22, 0.18) * entries
    return jnp.clip(entries, min=-most, max=most).astype(kind)


def setup_inputs(seed: int = 0) -> dict:
    streams_of = jax.random.split(jax.random.key(seed), 8)
    tokens = bell_draw(streams_of[0], (TOKENS, D), 1.0, 6.0, ((0, 32),))
    routes = draw_routes(jax.random.fold_in(streams_of[7], 71), 0)
    gate_values = jnp.clip(jnp.exp(math.log(1.0) - 2.3025851 * jax.random.uniform(streams_of[2], (HOMES, EXPERTS, SLOT), jnp.float32) ** block_levels(streams_of[2], (HOMES, EXPERTS, SLOT), ((0, 32),), -0.2, 0.2)), 0.1, 1.0)
    gate_weight = bell_draw(streams_of[3], (N_EXPERT, D, HID_DEV), D ** -0.5, 0.09375, ((0, 16), (1, 2)))
    up_weight = bell_draw(streams_of[4], (N_EXPERT, D, HID_DEV), D ** -0.5, 0.09375, ((0, 16), (1, 2)))
    down_weight = bell_draw(streams_of[5], (N_EXPERT, D, HID_DEV), FF ** -0.5, 0.125, ((0, 16), (1, 2)))
    cotangent = bell_draw(streams_of[6], (TOKENS, D), 1.0, 6.0, ((0, 32),))
    return dict(tokens=tokens, routes=routes, gate_values=gate_values, gate_weight=gate_weight, up_weight=up_weight, down_weight=down_weight, cotangent=cotangent)


def expert_pass(token_rows, cot_rows, gate_parts, up_parts, down_parts):
    rows_wide = token_rows.astype(jnp.float32)
    cot_wide = cot_rows.astype(jnp.float32)
    gate_wide = gate_parts.astype(jnp.float32)
    up_wide = up_parts.astype(jnp.float32)
    down_wide = down_parts.astype(jnp.float32)
    gate_pre = jnp.einsum('rd,sdh->rsh', rows_wide, gate_wide)
    up_pre = jnp.einsum('rd,sdh->rsh', rows_wide, up_wide)
    gate_sigma = jax.nn.sigmoid(gate_pre)
    hidden = (gate_pre * gate_sigma * up_pre).astype(jnp.bfloat16)
    part_out = jnp.einsum('rsh,sdh->srd', hidden.astype(jnp.float32), down_wide).astype(jnp.bfloat16)
    expert_out = jnp.sum(part_out.astype(jnp.float32), axis=0)
    hidden_grad = jnp.einsum('rd,sdh->rsh', cot_wide, down_wide)
    gate_rows = (hidden_grad * up_pre * gate_sigma * (1.0 + gate_pre * (1.0 - gate_sigma))).astype(jnp.bfloat16)
    up_rows = (hidden_grad * gate_pre * gate_sigma).astype(jnp.bfloat16)
    gate_rows_wide = gate_rows.astype(jnp.float32)
    up_rows_wide = up_rows.astype(jnp.float32)
    part_grad = (jnp.einsum('rsh,sdh->srd', gate_rows_wide, gate_wide) + jnp.einsum('rsh,sdh->srd', up_rows_wide, up_wide)).astype(jnp.bfloat16)
    row_grad = jnp.sum(part_grad.astype(jnp.float32), axis=0)
    gate_term = jnp.einsum('rd,rsh->sdh', rows_wide, gate_rows_wide)
    up_term = jnp.einsum('rd,rsh->sdh', rows_wide, up_rows_wide)
    down_term = jnp.einsum('rd,rsh->sdh', cot_wide, hidden.astype(jnp.float32))
    return expert_out, row_grad, gate_term, up_term, down_term


def reference(tokens, routes, gate_values, gate_weight, up_weight, down_weight, cotangent):
    token_blocks = tokens.reshape(N_DP, N_EXPERT, TOK_DEV, D)
    cot_blocks = cotangent.reshape(N_DP, N_EXPERT, TOK_DEV, D)
    route_blocks = routes.reshape(N_DP, N_EXPERT, EXPERTS, SLOT)
    scale_blocks = gate_values.reshape(N_DP, N_EXPERT, EXPERTS, SLOT)
    gate_parts = gate_weight.reshape(EXPERTS, SPLIT, D, HID_DEV)
    up_parts = up_weight.reshape(EXPERTS, SPLIT, D, HID_DEV)
    down_parts = down_weight.reshape(EXPERTS, SPLIT, D, HID_DEV)
    layer_out = jnp.zeros((N_DP, N_EXPERT, TOK_DEV, D), jnp.float32)
    token_grad = jnp.zeros((N_DP, N_EXPERT, TOK_DEV, D), jnp.float32)
    gate_grad = jnp.zeros((EXPERTS, SPLIT, D, HID_DEV), jnp.float32)
    up_grad = jnp.zeros((EXPERTS, SPLIT, D, HID_DEV), jnp.float32)
    down_grad = jnp.zeros((EXPERTS, SPLIT, D, HID_DEV), jnp.float32)
    home_index = jnp.arange(N_EXPERT).astype(jnp.int32)[:, None]
    for batch_index in range(N_DP):
        for expert_index in range(EXPERTS):
            chosen = route_blocks[batch_index, :, expert_index, :].astype(jnp.int32)
            scales = scale_blocks[batch_index, :, expert_index, :][:, :, None]
            picked = token_blocks[batch_index][home_index, chosen]
            cot_picked = (scales * cot_blocks[batch_index][home_index, chosen].astype(jnp.float32)).astype(jnp.bfloat16)
            expert_out, row_grad, gate_term, up_term, down_term = expert_pass(
                picked.reshape(-1, D), cot_picked.reshape(-1, D),
                gate_parts[expert_index], up_parts[expert_index], down_parts[expert_index])
            layer_out = layer_out.at[batch_index, home_index, chosen].add(scales * expert_out.reshape(N_EXPERT, SLOT, D))
            token_grad = token_grad.at[batch_index, home_index, chosen].add(row_grad.reshape(N_EXPERT, SLOT, D))
            gate_grad = gate_grad.at[expert_index].add(gate_term)
            up_grad = up_grad.at[expert_index].add(up_term)
            down_grad = down_grad.at[expert_index].add(down_term)
    return (layer_out.reshape(TOKENS, D).astype(jnp.bfloat16),
            token_grad.reshape(TOKENS, D).astype(jnp.bfloat16),
            gate_grad.reshape(N_EXPERT, D, HID_DEV).astype(jnp.bfloat16),
            up_grad.reshape(N_EXPERT, D, HID_DEV).astype(jnp.bfloat16),
            down_grad.reshape(N_EXPERT, D, HID_DEV).astype(jnp.bfloat16))
```

```python
import functools

import jax
import jax.numpy as jnp
from jax import lax
from jax.experimental import pallas as pl
from jax.experimental.pallas import tpu as pltpu
from jax.sharding import PartitionSpec as P

SPLIT = 8
BF = jnp.bfloat16
F32 = jnp.float32
AXES = ("dp", "expert")
NT = (((1,), (1,)), ((), ()))
TN = (((0,), (0,)), ((), ()))
VMEM_LIMIT = 48 * 1024 * 1024


def mm(a, b, dims=None):
    if dims is None:
        return jnp.dot(a, b, preferred_element_type=F32)
    return lax.dot_general(a, b, dims, preferred_element_type=F32)


def call(body, out_shape, n_smem, n_vmem, flops=0, moved=0, scratch=()):
    specs = [pl.BlockSpec(memory_space=pltpu.SMEM)] * n_smem
    specs += [pl.BlockSpec(memory_space=pltpu.VMEM)] * n_vmem
    return pl.pallas_call(
        body,
        out_shape=out_shape,
        in_specs=specs,
        out_specs=jax.tree.map(lambda _: pl.BlockSpec(memory_space=pltpu.VMEM), out_shape),
        scratch_shapes=list(scratch),
        compiler_params=pltpu.CompilerParams(vmem_limit_bytes=VMEM_LIMIT),
        cost_estimate=pl.CostEstimate(flops=flops, bytes_accessed=moved, transcendentals=0),
    )


def slot_values(read, count, slots, expert, experts, axis):
    shape = (count, 1) if axis == 0 else (1, count)
    place = lax.broadcasted_iota(jnp.int32, shape, axis)
    value = None
    for k in range(experts):
        e = lax.rem(expert + k, experts)
        for j in range(2 * slots):
            here = read(e, j % slots)
            if value is None:
                value = jnp.full(shape, here)
            else:
                value = jnp.where(place == k * 2 * slots + j, here, value)
    return value


def own_expert(experts):
    return lax.div(lax.axis_index("expert"), SPLIT)


def gather_body(n_dp, experts, slots, routes, gates, tokens, cot, *outs):
    batch = lax.axis_index("dp")
    expert = own_expert(experts)
    count = 2 * slots * experts
    block = tokens.shape[0]
    half = tokens.shape[1] // n_dp
    pos = slot_values(lambda e, s: routes[e, s], count, slots, expert, experts, 0)
    gate = slot_values(lambda e, s: gates[e, s], count, slots, expert, experts, 0)
    is_token = lax.rem(lax.broadcasted_iota(jnp.int32, (count, 1), 0), 2 * slots) < slots
    scale = jnp.where(is_token, 1.0, gate)
    hit = lax.broadcasted_iota(jnp.int32, (count, block), 1) == pos
    pick_token = jnp.where(hit & is_token, 1.0, 0.0).astype(BF)
    pick_cot = jnp.where(hit & ~is_token, 1.0, 0.0).astype(BF)
    for dx in range(n_dp):
        at = pl.ds(pl.multiple_of(lax.rem(batch + dx, n_dp) * half, 128), half)
        rows = mm(pick_token, tokens[:, at]) + mm(pick_cot, cot[:, at])
        rows = (rows * scale).astype(BF)
        for k in range(experts):
            outs[dx * experts + k][...] = rows[k * 2 * slots : (k + 1) * 2 * slots]


def arrange_body(n_dp, experts, slots, *refs):
    *msgs, out, wide = refs
    batch = lax.axis_index("dp")
    each = 2 * slots
    total = each * n_dp * experts
    for m, msg in enumerate(msgs):
        wide[m * each : (m + 1) * each, :] = msg[...].astype(F32)
    r = lax.broadcasted_iota(jnp.int32, (total, 1), 0)
    kind, rest = lax.div(r, total // 2), lax.rem(r, total // 2)
    b, rest = lax.div(rest, experts * slots), lax.rem(rest, experts * slots)
    k, s = lax.div(rest, slots), lax.rem(rest, slots)
    dx = lax.rem(batch - b + n_dp, n_dp)
    source = (dx * experts + k) * each + kind * slots + s
    pick = lax.broadcasted_iota(jnp.int32, (total, total), 1) == source
    out[...] = mm(jnp.where(pick, 1.0, 0.0).astype(BF), wide[...].astype(BF)).astype(BF)


def forward_body(*refs):
    *pieces, wg, wu, wd, xs, ys, part, part_sent = refs
    n = pieces[0].shape[0] // 2
    hid = wg.shape[2]
    for q, piece in enumerate(pieces):
        xs[q * n : (q + 1) * n, :] = piece[:n, :]
        ys[q * n : (q + 1) * n, :] = piece[n:, :]
    for i, (rows, w) in enumerate(((xs, wg), (xs, wu), (ys, wd))):
        got = mm(rows[...], w[0])
        part[:, i * hid : (i + 1) * hid] = got
        part_sent[:, i * hid : (i + 1) * hid] = got.astype(BF)


def backward_body(n_recv, *refs):
    part, *rest = refs
    recv, rest = rest[:n_recv], rest[n_recv:]
    wg, wu, wd, hidden, rows_a, rows_b, own, sib = rest
    hid = wg.shape[2]
    total = part[...]
    for other in recv:
        total = total + other[...].astype(F32)
    g, u, q = total[:, :hid], total[:, hid : 2 * hid], total[:, 2 * hid :]
    sig = jax.nn.sigmoid(g)
    h = (g * sig * u).astype(BF)
    a = (q * u * sig * (1.0 + g * (1.0 - sig))).astype(BF)
    b = (q * g * sig).astype(BF)
    hidden[...] = h
    rows_a[...] = a
    rows_b[...] = b
    p = mm(h, wd[0], NT).astype(BF)
    e = (mm(a, wg[0], NT) + mm(b, wu[0], NT)).astype(BF)
    n = part.shape[0] // SPLIT
    for piece in range(SPLIT):
        out = own if piece % 2 == 0 else sib
        at = (piece // 2) * 2 * n
        out[at : at + n, :] = p[piece * n : (piece + 1) * n]
        out[at + n : at + 2 * n, :] = e[piece * n : (piece + 1) * n]


def pair_sum_body(own, got, *outs):
    n = own.shape[0] // len(outs)
    for j, out in enumerate(outs):
        at = slice(j * n, (j + 1) * n)
        out[...] = (own[at, :].astype(F32) + got[at, :].astype(F32)).astype(BF)


def return_body(n_dp, experts, slots, n_in, *refs):
    ins, outs = refs[:n_in], refs[n_in:]
    batch = lax.axis_index("dp")
    each = 2 * slots
    total = each * n_dp * experts
    value = ins[0][...].astype(F32)
    for other in ins[1:]:
        value = value + other[...].astype(F32)
    r = lax.broadcasted_iota(jnp.int32, (total, 1), 0)
    m, j = lax.div(r, each), lax.rem(r, each)
    dx, k = lax.div(m, experts), lax.rem(m, experts)
    kind, s = lax.div(j, slots), lax.rem(j, slots)
    b = lax.rem(batch - dx + n_dp, n_dp)
    source = kind * (total // 2) + (b * experts + k) * slots + s
    pick = lax.broadcasted_iota(jnp.int32, (total, total), 1) == source
    rows = mm(jnp.where(pick, 1.0, 0.0).astype(BF), value.astype(BF)).astype(BF)
    for i, out in enumerate(outs):
        out[...] = rows[i * each : (i + 1) * each]


def home_body(n_dp, experts, slots, routes, gates, *refs):
    *msgs, layer_out, token_grad, wide = refs
    batch = lax.axis_index("dp")
    expert = own_expert(experts)
    each = 2 * slots
    count = each * experts
    block = layer_out.shape[0]
    half = layer_out.shape[1] // n_dp
    pos = slot_values(lambda e, s: routes[e, s], count, slots, expert, experts, 1)
    gate = slot_values(lambda e, s: gates[e, s], count, slots, expert, experts, 0)
    is_out = lax.rem(lax.broadcasted_iota(jnp.int32, (count, 1), 0), each) < slots
    is_out_lane = lax.rem(lax.broadcasted_iota(jnp.int32, (1, count), 1), each) < slots
    scale = jnp.where(is_out, gate, 1.0)
    hit = lax.broadcasted_iota(jnp.int32, (block, count), 0) == pos
    put_out = jnp.where(hit & is_out_lane, 1.0, 0.0).astype(BF)
    put_grad = jnp.where(hit & ~is_out_lane, 1.0, 0.0).astype(BF)
    for dx in range(n_dp):
        at = pl.ds(pl.multiple_of(lax.rem(batch + dx, n_dp) * half, 128), half)
        for k in range(experts):
            wide[k * each : (k + 1) * each, :] = msgs[dx * experts + k][...].astype(F32)
        value = wide[...] * scale
        high = value.astype(BF)
        low = (value - high.astype(F32)).astype(BF)
        layer_out[:, at] = (mm(put_out, high) + mm(put_out, low)).astype(BF)
        token_grad[:, at] = mm(put_grad, high).astype(BF)


def grads_body(xs, ys, rows_a, rows_b, hidden, gate_grad, up_grad, down_grad):
    gate_grad[0] = mm(xs[...], rows_a[...], TN).astype(BF)
    up_grad[0] = mm(xs[...], rows_b[...], TN).astype(BF)
    down_grad[0] = mm(ys[...], hidden[...], TN).astype(BF)


def shards(n_dp, n_exp, tokens, routes, gate_values, wg, wu, wd, cot):
    block, width = tokens.shape
    experts = routes.shape[1]
    slots = routes.shape[2]
    hid = wg.shape[2]
    half = width // n_dp
    each = 2 * slots
    block_rows = each * n_dp * experts
    n_rows = block_rows // 2 * SPLIT
    n_msg = n_dp * experts
    sds = jax.ShapeDtypeStruct

    def home_perm(dx, k, sign):
        return [
            (
                d * n_exp + i,
                (d + sign * dx) % n_dp * n_exp + (i // SPLIT + sign * k) % experts * SPLIT + i % SPLIT,
            )
            for d in range(n_dp)
            for i in range(n_exp)
        ]

    def part_perm(q):
        return [(d * n_exp + i, d * n_exp + (i ^ q)) for d in range(n_dp) for i in range(n_exp)]

    def batch_perm(dx):
        return [
            (d * n_exp + i, (d + dx) % n_dp * n_exp + i) for d in range(n_dp) for i in range(n_exp)
        ]

    def send(x, perm):
        return lax.ppermute(x, AXES, perm)

    kinds = [(dx, k) for dx in range(n_dp) for k in range(experts)]
    small = [sds((each, half), BF)] * n_msg
    msgs = call(
        functools.partial(gather_body, n_dp, experts, slots), small, 2, 2, moved=4 * block * width
    )(routes[0], gate_values[0], tokens, cot)
    got = [m if kind == (0, 0) else send(m, home_perm(*kind, 1)) for kind, m in zip(kinds, msgs)]
    piece = call(
        functools.partial(arrange_body, n_dp, experts, slots),
        sds((block_rows, half), BF),
        0,
        n_msg,
        scratch=[pltpu.VMEM((block_rows, half), F32)],
    )(*got)
    pieces = [None] * SPLIT
    for q in range(0, SPLIT, 2):
        pieces[q] = piece if q == 0 else send(piece, part_perm(q))
        pieces[q + 1] = send(pieces[q], part_perm(1))
    xs, ys, part, part_sent = call(
        forward_body,
        [
            sds((n_rows, half), BF),
            sds((n_rows, half), BF),
            sds((n_rows, 3 * hid), F32),
            sds((n_rows, 3 * hid), BF),
        ],
        0,
        SPLIT + 3,
    )(*pieces, wg, wu, wd)
    recv = [send(part_sent, batch_perm(dx)) for dx in range(1, n_dp)]
    hidden, rows_a, rows_b, own, sib = call(
        functools.partial(backward_body, n_dp - 1),
        [sds((n_rows, hid), BF)] * 3 + [sds((n_rows, half), BF)] * 2,
        0,
        n_dp + 3,
    )(part, *recv, wg, wu, wd)
    sums = call(pair_sum_body, [sds((block_rows, half), BF)] * (SPLIT // 2), 0, 2)(
        own, send(sib, part_perm(1))
    )
    back = [sums[0]] + [send(sums[j], part_perm(2 * j)) for j in range(1, SPLIT // 2)]
    gate_grad, up_grad, down_grad = call(
        grads_body,
        [sds((1, half, hid), BF)] * 3,
        0,
        5,
        flops=6 * n_rows * half * hid,
        moved=6 * half * hid,
    )(xs, ys, rows_a, rows_b, hidden)
    msgs = call(
        functools.partial(return_body, n_dp, experts, slots, len(back)), small, 0, len(back)
    )(*back)
    got = [m if kind == (0, 0) else send(m, home_perm(*kind, -1)) for kind, m in zip(kinds, msgs)]
    layer_out, token_grad = call(
        functools.partial(home_body, n_dp, experts, slots),
        [sds((block, width), BF)] * 2,
        2,
        n_msg,
        scratch=[pltpu.VMEM((each * experts, half), F32)],
    )(routes[0], gate_values[0], *got)
    return layer_out, token_grad, gate_grad, up_grad, down_grad


def solution(mesh):
    rows = P(AXES, None)
    slots = P(AXES, None, None)
    weights = P("expert", "dp", None)
    return jax.shard_map(
        functools.partial(shards, mesh.shape["dp"], mesh.shape["expert"]),
        mesh=mesh,
        in_specs=(rows, slots, slots, weights, weights, weights, rows),
        out_specs=(rows, rows, weights, weights, weights),
        check_vma=False,
    )
```

```python
import functools
import math

import jax
import jax.numpy as jnp
from jax import lax
from jax.experimental import pallas as pl
from jax.experimental.pallas import tpu as pltpu
from jax.sharding import PartitionSpec as P

SPLIT = 8
BF = jnp.bfloat16
F32 = jnp.float32
AXES = ("dp", "expert")
NT = (((1,), (1,)), ((), ()))
TN = (((0,), (0,)), ((), ()))
ANY = pl.BlockSpec(memory_space=pl.ANY)
HBM = pl.BlockSpec(memory_space=pltpu.HBM)
SMEM = pl.BlockSpec(memory_space=pltpu.SMEM)
VMEM = pl.BlockSpec(memory_space=pltpu.VMEM)


def mm(a, b, dims=None):
    if dims is None:
        return jnp.dot(a, b, preferred_element_type=F32)
    return lax.dot_general(a, b, dims, preferred_element_type=F32)


def in_hbm(x):
    return pltpu.with_memory_space_constraint(x, pltpu.HBM)


def size(x):
    return math.prod(x.shape) * jnp.dtype(x.dtype).itemsize


def call(
    body,
    out_shape,
    args,
    in_specs=None,
    out_specs=None,
    scratch=(),
    extra=0,
    after=(),
    mark=False,
    cost=None,
):
    n_in, n_out = len(args), len(out_shape)
    used = sum(map(size, args)) + sum(map(size, out_shape)) + extra
    in_specs = in_specs or [VMEM] * n_in
    out_specs = out_specs or [VMEM] * n_out

    def whole(*refs):
        ins, rest = refs[:n_in], refs[n_in + len(after) :]
        outs, rest = rest[:n_out], rest[n_out:]
        if mark:
            rest[0][...] = jnp.zeros_like(rest[0])
            rest = rest[1:]
        body(*ins, *outs, *rest)

    return pl.pallas_call(
        whole,
        out_shape=[*out_shape, *[jax.ShapeDtypeStruct((8, 128), F32)] * mark],
        in_specs=[*in_specs, *[ANY] * len(after)],
        out_specs=[*out_specs, *[VMEM] * mark],
        scratch_shapes=list(scratch),
        compiler_params=pltpu.CompilerParams(vmem_limit_bytes=min(2 * used + (4 << 20), 56 << 20)),
        cost_estimate=cost,
    )(*args, *after)


def slot_values(read, count, slots, expert, experts, axis):
    shape = (count, 1) if axis == 0 else (1, count)
    place = lax.broadcasted_iota(jnp.int32, shape, axis)
    value = None
    for k in range(experts):
        e = lax.rem(expert + k, experts)
        for j in range(2 * slots):
            here = read(e, j % slots)
            if value is None:
                value = jnp.full(shape, here)
            else:
                value = jnp.where(place == k * 2 * slots + j, here, value)
    return value


def own_expert(experts):
    return lax.div(lax.axis_index("expert"), SPLIT)


def gather_body(n_dp, experts, slots, routes_in, gates_in, tokens, cot, *refs):
    *outs, both, routes, gates, sems = refs
    batch = lax.axis_index("dp")
    expert = own_expert(experts)
    count = 2 * slots * experts
    block = tokens.shape[0]
    half = tokens.shape[1] // n_dp
    moves = [(routes_in, routes), (gates_in, gates)]
    for dx in range(n_dp):
        at = pl.ds(pl.multiple_of(lax.rem(batch + dx, n_dp) * half, 128), half)
        for i, src in enumerate((tokens, cot)):
            moves.append((src.at[:, at], both.at[dx, pl.ds(i * block, block)]))
    copies = [pltpu.make_async_copy(*move, sems.at[i]) for i, move in enumerate(moves)]
    for copy in copies:
        copy.start()
    for copy in copies[:2]:
        copy.wait()
    pos = slot_values(lambda e, s: routes[e, s], count, slots, expert, experts, 0)
    gate = slot_values(lambda e, s: gates[e, s], count, slots, expert, experts, 0)
    is_token = lax.rem(lax.broadcasted_iota(jnp.int32, (count, 1), 0), 2 * slots) < slots
    scale = jnp.where(is_token, 1.0, gate)
    row = jnp.where(is_token, pos, pos + block)
    hit = lax.broadcasted_iota(jnp.int32, (count, 2 * block), 1) == row
    pick = jnp.where(hit, 1.0, 0.0).astype(BF)
    for dx in range(n_dp):
        for copy in copies[2 + 2 * dx : 4 + 2 * dx]:
            copy.wait()
        rows = (mm(pick, both[dx]) * scale).astype(BF)
        for k in range(experts):
            outs[dx * experts + k][...] = rows[k * 2 * slots : (k + 1) * 2 * slots]


def row_map(n_dp, ks, slots, batch, to_block):
    each = 2 * slots
    total = each * n_dp * ks
    r = lax.broadcasted_iota(jnp.int32, (total, 1), 0)
    if to_block:
        kind, rest = lax.div(r, total // 2), lax.rem(r, total // 2)
        b, rest = lax.div(rest, ks * slots), lax.rem(rest, ks * slots)
        k, s = lax.div(rest, slots), lax.rem(rest, slots)
        dx = lax.rem(batch - b + n_dp, n_dp)
        source = (dx * ks + k) * each + kind * slots + s
    else:
        m, j = lax.div(r, each), lax.rem(r, each)
        dx, k = lax.div(m, ks), lax.rem(m, ks)
        kind, s = lax.div(j, slots), lax.rem(j, slots)
        b = lax.rem(batch - dx + n_dp, n_dp)
        source = kind * (total // 2) + (b * ks + k) * slots + s
    pick = lax.broadcasted_iota(jnp.int32, (total, total), 1) == source
    return jnp.where(pick, 1.0, 0.0).astype(BF)


def arrange_body(n_dp, experts, slots, order, *refs):
    *msgs, out, wide = refs
    each = 2 * slots
    for m, msg in zip(order, msgs):
        wide[m * each : (m + 1) * each, :] = msg[...].astype(F32)
    pick = row_map(n_dp, experts, slots, lax.axis_index("dp"), True)
    out[...] = mm(pick, wide[...].astype(BF)).astype(BF)


def load_body(src, dst, sem):
    copy = pltpu.make_async_copy(src, dst, sem)
    copy.start()
    copy.wait()


def forward_body(*refs):
    *pieces, wg, wu, wd, xs, ys, part, part_sent = refs
    n = pieces[0].shape[0] // 2
    hid = wg.shape[2]
    for q, piece in enumerate(pieces):
        xs[q * n : (q + 1) * n, :] = piece[:n, :]
        ys[q * n : (q + 1) * n, :] = piece[n:, :]
    for i, (rows, w) in enumerate(((xs, wg), (xs, wu), (ys, wd))):
        got = mm(rows[...], w[0])
        part[:, i * hid : (i + 1) * hid] = got
        part_sent[:, i * hid : (i + 1) * hid] = got.astype(BF)


def backward_body(n_recv, *refs):
    part, *rest = refs
    recv, rest = rest[:n_recv], rest[n_recv:]
    wg, wu, wd, rows_h, rows_a, rows_b, own, sib = rest
    hid = wg.shape[2]
    total = part[...]
    for other in recv:
        total = total + other[...].astype(F32)
    g, u, q = total[:, :hid], total[:, hid : 2 * hid], total[:, 2 * hid :]
    sig = jax.nn.sigmoid(g)
    h = (g * sig * u).astype(BF)
    a = (q * u * sig * (1.0 + g * (1.0 - sig))).astype(BF)
    b = (q * g * sig).astype(BF)
    rows_h[...] = h
    rows_a[...] = a
    rows_b[...] = b
    p = mm(h, wd[0], NT).astype(BF)
    e = (mm(a, wg[0], NT) + mm(b, wu[0], NT)).astype(BF)
    n = part.shape[0] // SPLIT
    for piece in range(SPLIT):
        out = own if piece % 2 == 0 else sib
        at = (piece // 2) * 2 * n
        out[at : at + n, :] = p[piece * n : (piece + 1) * n]
        out[at + n : at + 2 * n, :] = e[piece * n : (piece + 1) * n]


def pair_sum_body(own, got, *outs):
    n = own.shape[0] // len(outs)
    for j, out in enumerate(outs):
        at = slice(j * n, (j + 1) * n)
        out[...] = (own[at, :].astype(F32) + got[at, :].astype(F32)).astype(BF)


def return_body(n_dp, ks, slots, n_in, order, *refs):
    ins, outs = refs[:n_in], refs[n_in:]
    each = 2 * slots
    value = ins[0][...].astype(F32)
    for other in ins[1:]:
        value = value + other[...].astype(F32)
    pick = row_map(n_dp, ks, slots, lax.axis_index("dp"), False)
    rows = mm(pick, value.astype(BF)).astype(BF)
    for m, out in zip(order, outs):
        out[...] = rows[m * each : (m + 1) * each]


def home_body(n_dp, experts, order, put_out, put_grad, scale, *refs):
    msgs, outs, (layer_half, grad_half, wide, sems) = refs[:-6], refs[-6:-4], refs[-4:]
    msgs = dict(zip(order, msgs))
    batch = lax.axis_index("dp")
    each = msgs[0].shape[0]
    half = layer_half.shape[2]
    copies = []
    for dx in range(n_dp):
        for k in range(experts):
            wide[k * each : (k + 1) * each, :] = msgs[dx * experts + k][...].astype(F32)
        at = pl.ds(pl.multiple_of(lax.rem(batch + dx, n_dp) * half, 128), half)
        value = wide[...] * scale[...]
        high = value.astype(BF)
        low = (value - high.astype(F32)).astype(BF)
        grad_half[dx] = mm(put_grad[...], high).astype(BF)
        copies.append(pltpu.make_async_copy(grad_half.at[dx], outs[1].at[:, at], sems.at[2 * dx]))
        copies[-1].start()
        layer_half[dx] = (mm(put_out[...], high) + mm(put_out[...], low)).astype(BF)
        copies.append(
            pltpu.make_async_copy(layer_half.at[dx], outs[0].at[:, at], sems.at[2 * dx + 1])
        )
        copies[-1].start()
    for copy in copies:
        copy.wait()


def grads_body(experts, slots, routes, gates, xs, ys, rows_a, rows_b, rows_h, *refs):
    *outs, put_out, put_grad, scale, held, sems = refs
    copies = []
    for i, (rows, w) in enumerate(((xs, rows_a), (xs, rows_b), (ys, rows_h))):
        held[i] = mm(rows[...], w[...], TN).astype(BF)
        copies.append(pltpu.make_async_copy(held.at[i], outs[i].at[0], sems.at[i]))
        copies[-1].start()
    expert = own_expert(experts)
    each = 2 * slots
    count = each * experts
    block = put_out.shape[0]
    pos = slot_values(lambda e, s: routes[e, s], count, slots, expert, experts, 1)
    gate = slot_values(lambda e, s: gates[e, s], count, slots, expert, experts, 0)
    is_out = lax.rem(lax.broadcasted_iota(jnp.int32, (count, 1), 0), each) < slots
    is_out_lane = lax.rem(lax.broadcasted_iota(jnp.int32, (1, count), 1), each) < slots
    scale[...] = jnp.where(is_out, gate, 1.0)
    hit = lax.broadcasted_iota(jnp.int32, (block, count), 0) == pos
    put_out[...] = jnp.where(hit & is_out_lane, 1.0, 0.0).astype(BF)
    put_grad[...] = jnp.where(hit & ~is_out_lane, 1.0, 0.0).astype(BF)
    for copy in copies:
        copy.wait()


def shards(n_dp, n_exp, tokens, routes, gate_values, wg, wu, wd, cot):
    block, width = tokens.shape
    experts = routes.shape[1]
    slots = routes.shape[2]
    hid = wg.shape[2]
    half = width // n_dp
    each = 2 * slots
    n_msg = n_dp * experts
    sds = jax.ShapeDtypeStruct

    def home_perm(dx, k, sign):
        return [
            (
                d * n_exp + i,
                (d + sign * dx) % n_dp * n_exp + (i // SPLIT + sign * k) % experts * SPLIT + i % SPLIT,
            )
            for d in range(n_dp)
            for i in range(n_exp)
        ]

    def part_perm(q):
        return [(d * n_exp + i, d * n_exp + (i ^ q)) for d in range(n_dp) for i in range(n_exp)]

    def batch_perm(dx):
        return [
            (d * n_exp + i, (d + dx) % n_dp * n_exp + i) for d in range(n_dp) for i in range(n_exp)
        ]

    def send(x, perm):
        return lax.ppermute(x, AXES, perm)

    kinds = [(dx, k) for dx in range(n_dp) for k in range(experts)]
    order = sorted(range(n_msg), key=lambda m: (kinds[m][1] == 0, kinds[m][0] == 0, m))
    small = [sds((each, half), BF)] * n_msg
    msgs = call(
        functools.partial(gather_body, n_dp, experts, slots),
        small,
        [in_hbm(x) for x in (routes[0], gate_values[0], tokens, cot)],
        in_specs=[HBM] * 4,
        scratch=[
            pltpu.VMEM((n_dp, 2 * block, half), BF),
            pltpu.SMEM((experts, slots), jnp.int32),
            pltpu.SMEM((experts, slots), F32),
            pltpu.SemaphoreType.DMA((2 + 2 * n_dp,)),
        ],
    )
    got = dict(zip(kinds, msgs))
    for kind in kinds[1:]:
        got[kind] = send(got[kind], home_perm(*kind, 1))
    down, mark = call(
        load_body,
        [sds(wd.shape, BF)],
        [in_hbm(wd)],
        in_specs=[HBM],
        scratch=[pltpu.SemaphoreType.DMA],
        mark=True,
    )
    rows = each * n_msg
    n_rows = rows // 2 * SPLIT
    (piece,) = call(
        functools.partial(arrange_body, n_dp, experts, slots, order),
        [sds((rows, half), BF)],
        [got[kinds[m]] for m in order],
        scratch=[pltpu.VMEM((rows, half), F32)],
        extra=rows * half * 8,
        after=[mark],
    )
    pieces = [None] * SPLIT
    for q in range(0, SPLIT, 2):
        pieces[q] = piece if q == 0 else send(piece, part_perm(q))
        pieces[q + 1] = send(pieces[q], part_perm(1))
    xs, ys, part, part_sent = call(
        forward_body,
        [
            sds((n_rows, half), BF),
            sds((n_rows, half), BF),
            sds((n_rows, 3 * hid), F32),
            sds((n_rows, 3 * hid), BF),
        ],
        (*pieces, wg, wu, down),
    )
    recv = [send(part_sent, batch_perm(dx)) for dx in range(1, n_dp)]
    rows_h, rows_a, rows_b, own, sib = call(
        functools.partial(backward_body, n_dp - 1),
        [sds((n_rows, hid), BF)] * 3 + [sds((n_rows, half), BF)] * 2,
        (part, *recv, wg, wu, down),
        extra=n_rows * half * 12,
    )
    sums = call(
        pair_sum_body, [sds((rows, half), BF)] * (SPLIT // 2), (own, send(sib, part_perm(1)))
    )
    back = [sums[0]] + [send(sums[j], part_perm(2 * j)) for j in range(1, SPLIT // 2)]
    count = each * experts
    *grads, put_out, put_grad, scale, mark = call(
        functools.partial(grads_body, experts, slots),
        [sds((1, half, hid), BF)] * 3 + [sds((block, count), BF)] * 2 + [sds((count, 1), F32)],
        (routes[0], gate_values[0], xs, ys, rows_a, rows_b, rows_h),
        in_specs=[SMEM] * 2 + [VMEM] * 5,
        out_specs=[HBM] * 3 + [VMEM] * 3,
        scratch=[pltpu.VMEM((3, half, hid), BF), pltpu.SemaphoreType.DMA((3,))],
        extra=n_rows * half * 4 + half * hid * 12,
        mark=True,
        cost=pl.CostEstimate(
            flops=6 * n_rows * half * hid, bytes_accessed=6 * half * hid, transcendentals=0
        ),
    )
    msgs = call(
        functools.partial(return_body, n_dp, experts, slots, len(back), order),
        [sds((each, half), BF)] * n_msg,
        back,
        extra=rows * half * 8,
        after=[mark],
    )
    got = {kinds[m]: msg for m, msg in zip(order, msgs)}
    for kind in kinds[1:]:
        got[kind] = send(got[kind], home_perm(*kind, -1))
    layer_out, token_grad = call(
        functools.partial(home_body, n_dp, experts, order),
        [sds((block, width), BF)] * 2,
        (put_out, put_grad, scale, *[got[kinds[m]] for m in order]),
        out_specs=[HBM] * 2,
        scratch=[pltpu.VMEM((n_dp, block, half), BF)] * 2
        + [pltpu.VMEM((count, half), F32), pltpu.SemaphoreType.DMA((2 * n_dp,))],
        extra=block * half * 16 + count * half * 4,
    )
    return layer_out, token_grad, *grads


def solution(mesh):
    rows = P(AXES, None)
    slots = P(AXES, None, None)
    weights = P("expert", "dp", None)
    return jax.shard_map(
        functools.partial(shards, mesh.shape["dp"], mesh.shape["expert"]),
        mesh=mesh,
        in_specs=(rows, slots, slots, weights, weights, weights, rows),
        out_specs=(rows, rows, weights, weights, weights),
        check_vma=False,
    )
```

```python
import functools
import math

import jax
import jax.numpy as jnp
from jax import lax
from jax.experimental import pallas as pl
from jax.experimental.pallas import tpu as pltpu
from jax.sharding import PartitionSpec as P

SPLIT = 8
BF = jnp.bfloat16
F32 = jnp.float32
AXES = ("dp", "expert")
NT = (((1,), (1,)), ((), ()))
TN = (((0,), (0,)), ((), ()))
ANY = pl.BlockSpec(memory_space=pl.ANY)
HBM = pl.BlockSpec(memory_space=pltpu.HBM)
VMEM = pl.BlockSpec(memory_space=pltpu.VMEM)


def mm(a, b, dims=None):
    if dims is None:
        return jnp.dot(a, b, preferred_element_type=F32)
    return lax.dot_general(a, b, dims, preferred_element_type=F32)


def in_hbm(x):
    return pltpu.with_memory_space_constraint(x, pltpu.HBM)


def size(x):
    return math.prod(x.shape) * jnp.dtype(x.dtype).itemsize


def call(
    body,
    out_shape,
    args,
    in_specs=None,
    out_specs=None,
    scratch=(),
    extra=0,
    after=(),
    mark=False,
    cost=None,
):
    n_in, n_out = len(args), len(out_shape)
    used = sum(map(size, args)) + sum(map(size, out_shape)) + extra
    in_specs = in_specs or [VMEM] * n_in
    out_specs = out_specs or [VMEM] * n_out

    def whole(*refs):
        ins, rest = refs[:n_in], refs[n_in + len(after) :]
        outs, rest = rest[:n_out], rest[n_out:]
        if mark:
            rest[0][...] = jnp.zeros_like(rest[0])
            rest = rest[1:]
        body(*ins, *outs, *rest)

    return pl.pallas_call(
        whole,
        out_shape=[*out_shape, *[jax.ShapeDtypeStruct((8, 128), F32)] * mark],
        in_specs=[*in_specs, *[ANY] * len(after)],
        out_specs=[*out_specs, *[VMEM] * mark],
        scratch_shapes=list(scratch),
        compiler_params=pltpu.CompilerParams(vmem_limit_bytes=min(2 * used + (4 << 20), 56 << 20)),
        cost_estimate=cost,
    )(*args, *after)


def slot_values(read, count, slots, expert, experts, axis):
    shape = (count, 1) if axis == 0 else (1, count)
    place = lax.broadcasted_iota(jnp.int32, shape, axis)
    value = None
    for k in range(experts):
        e = lax.rem(expert + k, experts)
        for j in range(2 * slots):
            here = read(e, j % slots)
            if value is None:
                value = jnp.full(shape, here)
            else:
                value = jnp.where(place == k * 2 * slots + j, here, value)
    return value


def own_expert(experts):
    return lax.div(lax.axis_index("expert"), SPLIT)


def gather_body(n_dp, experts, slots, routes_in, gates_in, tokens, cot, *refs):
    *outs, both, routes, gates, sems = refs
    batch = lax.axis_index("dp")
    expert = own_expert(experts)
    count = 2 * slots * experts
    block = tokens.shape[0]
    half = tokens.shape[1] // n_dp
    moves = [(routes_in, routes), (gates_in, gates)]
    for dx in range(n_dp):
        at = pl.ds(pl.multiple_of(lax.rem(batch + dx, n_dp) * half, 128), half)
        for i, src in enumerate((tokens, cot)):
            moves.append((src.at[:, at], both.at[dx, pl.ds(i * block, block)]))
    copies = [pltpu.make_async_copy(*move, sems.at[i]) for i, move in enumerate(moves)]
    for copy in copies:
        copy.start()
    for copy in copies[:2]:
        copy.wait()
    pos = slot_values(lambda e, s: routes[e, s], count, slots, expert, experts, 0)
    gate = slot_values(lambda e, s: gates[e, s], count, slots, expert, experts, 0)
    is_token = lax.rem(lax.broadcasted_iota(jnp.int32, (count, 1), 0), 2 * slots) < slots
    scale = jnp.where(is_token, 1.0, gate)
    row = jnp.where(is_token, pos, pos + block)
    hit = lax.broadcasted_iota(jnp.int32, (count, 2 * block), 1) == row
    pick = jnp.where(hit, 1.0, 0.0).astype(BF)
    for dx in range(n_dp):
        for copy in copies[2 + 2 * dx : 4 + 2 * dx]:
            copy.wait()
        rows = (mm(pick, both[dx]) * scale).astype(BF)
        for k in range(experts):
            outs[dx * experts + k][...] = rows[k * 2 * slots : (k + 1) * 2 * slots]


def row_map(n_dp, ks, slots, batch, to_block):
    each = 2 * slots
    total = each * n_dp * ks
    r = lax.broadcasted_iota(jnp.int32, (total, 1), 0)
    if to_block:
        kind, rest = lax.div(r, total // 2), lax.rem(r, total // 2)
        b, rest = lax.div(rest, ks * slots), lax.rem(rest, ks * slots)
        k, s = lax.div(rest, slots), lax.rem(rest, slots)
        dx = lax.rem(batch - b + n_dp, n_dp)
        source = (dx * ks + k) * each + kind * slots + s
    else:
        m, j = lax.div(r, each), lax.rem(r, each)
        dx, k = lax.div(m, ks), lax.rem(m, ks)
        kind, s = lax.div(j, slots), lax.rem(j, slots)
        b = lax.rem(batch - dx + n_dp, n_dp)
        source = kind * (total // 2) + (b * ks + k) * slots + s
    pick = lax.broadcasted_iota(jnp.int32, (total, total), 1) == source
    return jnp.where(pick, 1.0, 0.0).astype(BF)


def arrange_body(n_dp, experts, slots, order, *refs):
    *msgs, out, wide = refs
    each = 2 * slots
    for m, msg in zip(order, msgs):
        wide[m * each : (m + 1) * each, :] = msg[...].astype(F32)
    pick = row_map(n_dp, experts, slots, lax.axis_index("dp"), True)
    out[...] = mm(pick, wide[...].astype(BF)).astype(BF)


def load_body(experts, slots, src, routes_in, gates_in, dst, put_out, put_grad, scale, routes, gates, sems):
    moves = ((src, dst), (routes_in, routes), (gates_in, gates))
    copies = [pltpu.make_async_copy(*move, sems.at[i]) for i, move in enumerate(moves)]
    for copy in copies:
        copy.start()
    for copy in copies[1:]:
        copy.wait()
    expert = own_expert(experts)
    each = 2 * slots
    count = each * experts
    block = put_out.shape[0]
    pos = slot_values(lambda e, s: routes[e, s], count, slots, expert, experts, 1)
    gate = slot_values(lambda e, s: gates[e, s], count, slots, expert, experts, 0)
    is_out = lax.rem(lax.broadcasted_iota(jnp.int32, (count, 1), 0), each) < slots
    is_out_lane = lax.rem(lax.broadcasted_iota(jnp.int32, (1, count), 1), each) < slots
    scale[...] = jnp.where(is_out, gate, 1.0)
    hit = lax.broadcasted_iota(jnp.int32, (block, count), 0) == pos
    put_out[...] = jnp.where(hit & is_out_lane, 1.0, 0.0).astype(BF)
    put_grad[...] = jnp.where(hit & ~is_out_lane, 1.0, 0.0).astype(BF)
    copies[0].wait()


def forward_body(*refs):
    *pieces, wg, wu, wd, part, part_sent = refs
    n = pieces[0].shape[0] // 2
    hid = wg.shape[2]
    xs = jnp.concatenate([piece[:n, :] for piece in pieces], axis=0)
    ys = jnp.concatenate([piece[n:, :] for piece in pieces], axis=0)
    for i, (rows, w) in enumerate(((xs, wg), (xs, wu), (ys, wd))):
        got = mm(rows, w[0])
        part[:, i * hid : (i + 1) * hid] = got
        part_sent[:, i * hid : (i + 1) * hid] = got.astype(BF)


def backward_body(n_pieces, n_recv, *refs):
    part, *rest = refs
    recv, rest = rest[:n_recv], rest[n_recv:]
    wg, wu, wd, rows_h, rows_a, rows_b, own, sib = rest
    hid = wg.shape[2]
    total = part[...]
    for other in recv:
        total = total + other[...].astype(F32)
    g, u, q = total[:, :hid], total[:, hid : 2 * hid], total[:, 2 * hid :]
    sig = jax.nn.sigmoid(g)
    h = (g * sig * u).astype(BF)
    a = (q * u * sig * (1.0 + g * (1.0 - sig))).astype(BF)
    b = (q * g * sig).astype(BF)
    rows_h[...] = h
    rows_a[...] = a
    rows_b[...] = b
    p = mm(h, wd[0], NT).astype(BF)
    e = (mm(a, wg[0], NT) + mm(b, wu[0], NT)).astype(BF)
    n = part.shape[0] // n_pieces
    for i in range(n_pieces):
        out, at = (own, i) if 2 * i < n_pieces else (sib, i - n_pieces // 2)
        out[2 * at * n : (2 * at + 1) * n, :] = p[i * n : (i + 1) * n]
        out[(2 * at + 1) * n : (2 * at + 2) * n, :] = e[i * n : (i + 1) * n]


def pair_sum_body(own, got, *outs):
    n = own.shape[0] // len(outs)
    for j, out in enumerate(outs):
        at = slice(j * n, (j + 1) * n)
        out[...] = (own[at, :].astype(F32) + got[at, :].astype(F32)).astype(BF)


def return_body(n_dp, ks, slots, n_in, order, *refs):
    ins, outs = refs[:n_in], refs[n_in:]
    each = 2 * slots
    value = ins[0][...].astype(F32)
    for other in ins[1:]:
        value = value + other[...].astype(F32)
    pick = row_map(n_dp, ks, slots, lax.axis_index("dp"), False)
    rows = mm(pick, value.astype(BF)).astype(BF)
    for m, out in zip(order, outs):
        out[...] = rows[m * each : (m + 1) * each]


def home_body(n_dp, experts, order, put_out, put_grad, scale, *refs):
    msgs, outs, (layer_half, grad_half, wide, sems) = refs[:-6], refs[-6:-4], refs[-4:]
    msgs = dict(zip(order, msgs))
    batch = lax.axis_index("dp")
    each = msgs[0].shape[0]
    half = layer_half.shape[2]
    copies = []
    for dx in range(n_dp):
        for k in range(experts):
            wide[k * each : (k + 1) * each, :] = msgs[dx * experts + k][...].astype(F32)
        at = pl.ds(pl.multiple_of(lax.rem(batch + dx, n_dp) * half, 128), half)
        value = wide[...] * scale[...]
        high = value.astype(BF)
        low = (value - high.astype(F32)).astype(BF)
        grad_half[dx] = mm(put_grad[...], high).astype(BF)
        copies.append(pltpu.make_async_copy(grad_half.at[dx], outs[1].at[:, at], sems.at[2 * dx]))
        copies[-1].start()
        layer_half[dx] = (mm(put_out[...], high) + mm(put_out[...], low)).astype(BF)
        copies.append(
            pltpu.make_async_copy(layer_half.at[dx], outs[0].at[:, at], sems.at[2 * dx + 1])
        )
        copies[-1].start()
    for copy in copies:
        copy.wait()


def grads_body(*refs):
    pieces, lefts, (*outs, xs, ys, w, held, sems) = (
        refs[:SPLIT],
        refs[SPLIT : SPLIT + 6],
        refs[SPLIT + 6 :],
    )
    n = pieces[0].shape[0] // 2
    for i, piece in enumerate(pieces):
        xs[i * n : (i + 1) * n, :] = piece[:n, :]
        ys[i * n : (i + 1) * n, :] = piece[n:, :]
    copies = []
    for i, rows in enumerate((xs, xs, ys)):
        for j in range(2):
            left = lefts[3 * j + i]
            w[j * left.shape[0] : (j + 1) * left.shape[0], :] = left[...]
        held[i] = mm(rows[...], w[...], TN).astype(BF)
        copies.append(pltpu.make_async_copy(held.at[i], outs[i].at[0], sems.at[i]))
        copies[-1].start()
    for copy in copies:
        copy.wait()


def shards(n_dp, n_exp, tokens, routes, gate_values, wg, wu, wd, cot):
    block, width = tokens.shape
    experts = routes.shape[1]
    slots = routes.shape[2]
    hid = wg.shape[2]
    half = width // n_dp
    each = 2 * slots
    n_msg = n_dp * experts
    sds = jax.ShapeDtypeStruct

    def home_perm(dx, k, sign):
        return [
            (
                d * n_exp + i,
                (d + sign * dx) % n_dp * n_exp + (i // SPLIT + sign * k) % experts * SPLIT + i % SPLIT,
            )
            for d in range(n_dp)
            for i in range(n_exp)
        ]

    def part_perm(q):
        return [(d * n_exp + i, d * n_exp + (i ^ q)) for d in range(n_dp) for i in range(n_exp)]

    def batch_perm(dx):
        return [
            (d * n_exp + i, (d + dx) % n_dp * n_exp + i) for d in range(n_dp) for i in range(n_exp)
        ]

    def send(x, perm):
        return lax.ppermute(x, AXES, perm)

    kinds = [(dx, k) for dx in range(n_dp) for k in range(experts)]
    order = sorted(range(n_msg), key=lambda m: (kinds[m][1] == 0, kinds[m][0] == 0, m))
    small = [sds((each, half), BF)] * n_msg
    msgs = call(
        functools.partial(gather_body, n_dp, experts, slots),
        small,
        [in_hbm(x) for x in (routes[0], gate_values[0], tokens, cot)],
        in_specs=[HBM] * 4,
        scratch=[
            pltpu.VMEM((n_dp, 2 * block, half), BF),
            pltpu.SMEM((experts, slots), jnp.int32),
            pltpu.SMEM((experts, slots), F32),
            pltpu.SemaphoreType.DMA((2 + 2 * n_dp,)),
        ],
    )
    got = dict(zip(kinds, msgs))
    for kind in kinds[1:]:
        got[kind] = send(got[kind], home_perm(*kind, 1))
    count = each * experts
    small = [pltpu.SMEM((experts, slots), jnp.int32), pltpu.SMEM((experts, slots), F32)]
    down, put_out, put_grad, scale, mark = call(
        functools.partial(load_body, experts, slots),
        [sds(wd.shape, BF)] + [sds((block, count), BF)] * 2 + [sds((count, 1), F32)],
        [in_hbm(x) for x in (wd, routes[0], gate_values[0])],
        in_specs=[HBM] * 3,
        scratch=[*small, pltpu.SemaphoreType.DMA((3,))],
        mark=True,
    )
    rows = each * n_msg
    n_rows = rows // 2 * SPLIT
    (piece,) = call(
        functools.partial(arrange_body, n_dp, experts, slots, order),
        [sds((rows, half), BF)],
        [got[kinds[m]] for m in order],
        scratch=[pltpu.VMEM((rows, half), F32)],
        extra=rows * half * 8,
        after=[mark],
    )
    own_pieces = [piece] + [send(piece, part_perm(q)) for q in range(2, SPLIT, 2)]
    sib_pieces = [send(p, part_perm(1)) for p in own_pieces]
    chips = SPLIT // 2
    halves = [(0, chips - 1), tuple(range(1, chips - 1))]
    ordered = [[own_pieces[j] for j in js] + [sib_pieces[j] for j in js] for js in halves]
    mark, parts, recv = (), [], []
    for i, pieces in enumerate(ordered):
        n = len(pieces) * rows // 2
        part, part_sent, *mark = call(
            forward_body,
            [sds((n, 3 * hid), F32), sds((n, 3 * hid), BF)],
            (*pieces, wg, wu, down),
            extra=2 * n * half * 2 + n * hid * 4,
            after=mark,
            mark=i == 0,
        )
        parts.append(part)
        recv.append([send(part_sent, batch_perm(dx)) for dx in range(1, n_dp)])
    lefts, sums, mark = [], {}, ()
    for i, js in enumerate(halves):
        n = parts[i].shape[0]
        rows_h, rows_a, rows_b, own, sib, *mark = call(
            functools.partial(backward_body, 2 * len(js), n_dp - 1),
            [sds((n, hid), BF)] * 3 + [sds((n, half), BF)] * 2,
            (parts[i], *recv[i], wg, wu, down),
            extra=n * half * 12,
            after=mark,
            mark=i == 0,
        )
        lefts += [rows_a, rows_b, rows_h]
        got = call(
            pair_sum_body, [sds((rows, half), BF)] * len(js), (own, send(sib, part_perm(1)))
        )
        sums.update(zip(js, got))
    back = [sums[0]] + [send(sums[j], part_perm(2 * j)) for js in halves for j in js if j]
    *grads, mark = call(
        grads_body,
        [sds((1, half, hid), BF)] * 3,
        (*ordered[0], *ordered[1], *lefts),
        out_specs=[HBM] * 3,
        scratch=[pltpu.VMEM((n_rows, half), BF)] * 2
        + [
            pltpu.VMEM((n_rows, hid), BF),
            pltpu.VMEM((3, half, hid), BF),
            pltpu.SemaphoreType.DMA((3,)),
        ],
        extra=n_rows * half * 8 + half * hid * 12,
        mark=True,
        cost=pl.CostEstimate(
            flops=6 * n_rows * half * hid, bytes_accessed=6 * half * hid, transcendentals=0
        ),
    )
    msgs = call(
        functools.partial(return_body, n_dp, experts, slots, len(back), order),
        [sds((each, half), BF)] * n_msg,
        back,
        extra=rows * half * 8,
        after=[mark],
    )
    got = {kinds[m]: msg for m, msg in zip(order, msgs)}
    for kind in kinds[1:]:
        got[kind] = send(got[kind], home_perm(*kind, -1))
    layer_out, token_grad = call(
        functools.partial(home_body, n_dp, experts, order),
        [sds((block, width), BF)] * 2,
        (put_out, put_grad, scale, *[got[kinds[m]] for m in order]),
        out_specs=[HBM] * 2,
        scratch=[pltpu.VMEM((n_dp, block, half), BF)] * 2
        + [pltpu.VMEM((count, half), F32), pltpu.SemaphoreType.DMA((2 * n_dp,))],
        extra=block * half * 16 + count * half * 4,
    )
    return layer_out, token_grad, *grads


def solution(mesh):
    rows = P(AXES, None)
    slots = P(AXES, None, None)
    weights = P("expert", "dp", None)
    return jax.shard_map(
        functools.partial(shards, mesh.shape["dp"], mesh.shape["expert"]),
        mesh=mesh,
        in_specs=(rows, slots, slots, weights, weights, weights, rows),
        out_specs=(rows, rows, weights, weights, weights),
        check_vma=False,
    )
```

```python
import functools
import math

import jax
import jax.numpy as jnp
from jax import lax
from jax.experimental import pallas as pl
from jax.experimental.pallas import tpu as pltpu
from jax.sharding import PartitionSpec as P

SPLIT = 8
BF = jnp.bfloat16
F32 = jnp.float32
AXES = ("dp", "expert")
TN = (((0,), (0,)), ((), ()))
ANY = pl.BlockSpec(memory_space=pl.ANY)
HBM = pl.BlockSpec(memory_space=pltpu.HBM)
VMEM = pl.BlockSpec(memory_space=pltpu.VMEM)


def mm(a, b, dims=None):
    if dims is None:
        return jnp.dot(a, b, preferred_element_type=F32)
    return lax.dot_general(a, b, dims, preferred_element_type=F32)


def in_hbm(x):
    return pltpu.with_memory_space_constraint(x, pltpu.HBM)


def size(x):
    return math.prod(x.shape) * jnp.dtype(x.dtype).itemsize


def call(
    body,
    out_shape,
    args,
    in_specs=None,
    out_specs=None,
    scratch=(),
    extra=0,
    after=(),
    mark=False,
    cost=None,
):
    n_in, n_out = len(args), len(out_shape)
    used = sum(map(size, args)) + sum(map(size, out_shape)) + extra
    in_specs = in_specs or [VMEM] * n_in
    out_specs = out_specs or [VMEM] * n_out

    def whole(*refs):
        ins, rest = refs[:n_in], refs[n_in + len(after) :]
        outs, rest = rest[:n_out], rest[n_out:]
        if mark:
            rest[0][...] = jnp.zeros_like(rest[0])
            rest = rest[1:]
        body(*ins, *outs, *rest)

    return pl.pallas_call(
        whole,
        out_shape=[*out_shape, *[jax.ShapeDtypeStruct((8, 128), F32)] * mark],
        in_specs=[*in_specs, *[ANY] * len(after)],
        out_specs=[*out_specs, *[VMEM] * mark],
        scratch_shapes=list(scratch),
        compiler_params=pltpu.CompilerParams(vmem_limit_bytes=min(2 * used + (4 << 20), 56 << 20)),
        cost_estimate=cost,
    )(*args, *after)


def slot_values(read, count, slots, expert, experts, axis):
    shape = (count, 1) if axis == 0 else (1, count)
    place = lax.broadcasted_iota(jnp.int32, shape, axis)
    value = None
    for k in range(experts):
        e = lax.rem(expert + k, experts)
        for j in range(2 * slots):
            here = read(e, j % slots)
            if value is None:
                value = jnp.full(shape, here)
            else:
                value = jnp.where(place == k * 2 * slots + j, here, value)
    return value


def own_expert(experts):
    return lax.div(lax.axis_index("expert"), SPLIT)


def gather_body(n_dp, experts, slots, routes_in, gates_in, tokens, cot, *refs):
    *outs, both, routes, gates, sems = refs
    batch = lax.axis_index("dp")
    expert = own_expert(experts)
    count = 2 * slots * experts
    block = tokens.shape[0]
    half = tokens.shape[1] // n_dp
    moves = [(routes_in, routes), (gates_in, gates)]
    for dx in range(n_dp):
        at = pl.ds(pl.multiple_of(lax.rem(batch + dx, n_dp) * half, 128), half)
        for i, src in enumerate((tokens, cot)):
            moves.append((src.at[:, at], both.at[dx, pl.ds(i * block, block)]))
    copies = [pltpu.make_async_copy(*move, sems.at[i]) for i, move in enumerate(moves)]
    for copy in copies:
        copy.start()
    for copy in copies[:2]:
        copy.wait()
    pos = slot_values(lambda e, s: routes[e, s], count, slots, expert, experts, 0)
    gate = slot_values(lambda e, s: gates[e, s], count, slots, expert, experts, 0)
    is_token = lax.rem(lax.broadcasted_iota(jnp.int32, (count, 1), 0), 2 * slots) < slots
    scale = jnp.where(is_token, 1.0, gate)
    row = jnp.where(is_token, pos, pos + block)
    hit = lax.broadcasted_iota(jnp.int32, (count, 2 * block), 1) == row
    pick = jnp.where(hit, 1.0, 0.0).astype(BF)
    for dx in range(n_dp):
        for copy in copies[2 + 2 * dx : 4 + 2 * dx]:
            copy.wait()
        rows = (mm(pick, both[dx]) * scale).astype(BF)
        for k in range(experts):
            outs[dx * experts + k][...] = rows[k * 2 * slots : (k + 1) * 2 * slots]


def row_map(n_dp, ks, slots, batch, to_block):
    each = 2 * slots
    total = each * n_dp * ks
    r = lax.broadcasted_iota(jnp.int32, (total, 1), 0)
    if to_block:
        kind, rest = lax.div(r, total // 2), lax.rem(r, total // 2)
        b, rest = lax.div(rest, ks * slots), lax.rem(rest, ks * slots)
        k, s = lax.div(rest, slots), lax.rem(rest, slots)
        dx = lax.rem(batch - b + n_dp, n_dp)
        source = (dx * ks + k) * each + kind * slots + s
    else:
        m, j = lax.div(r, each), lax.rem(r, each)
        dx, k = lax.div(m, ks), lax.rem(m, ks)
        kind, s = lax.div(j, slots), lax.rem(j, slots)
        b = lax.rem(batch - dx + n_dp, n_dp)
        source = kind * (total // 2) + (b * ks + k) * slots + s
    pick = lax.broadcasted_iota(jnp.int32, (total, total), 1) == source
    return jnp.where(pick, 1.0, 0.0).astype(BF)


def arrange_body(n_dp, experts, slots, order, *refs):
    *msgs, out, wide = refs
    each = 2 * slots
    for m, msg in zip(order, msgs):
        wide[m * each : (m + 1) * each, :] = msg[...].astype(F32)
    pick = row_map(n_dp, experts, slots, lax.axis_index("dp"), True)
    out[...] = mm(pick, wide[...].astype(BF)).astype(BF)


def load_body(experts, slots, src, routes_in, gates_in, dst, put_out, put_grad, scale, routes, gates, sems):
    moves = ((src, dst), (routes_in, routes), (gates_in, gates))
    copies = [pltpu.make_async_copy(*move, sems.at[i]) for i, move in enumerate(moves)]
    for copy in copies:
        copy.start()
    for copy in copies[1:]:
        copy.wait()
    expert = own_expert(experts)
    each = 2 * slots
    count = each * experts
    block = put_out.shape[0]
    pos = slot_values(lambda e, s: routes[e, s], count, slots, expert, experts, 1)
    gate = slot_values(lambda e, s: gates[e, s], count, slots, expert, experts, 0)
    is_out = lax.rem(lax.broadcasted_iota(jnp.int32, (count, 1), 0), each) < slots
    is_out_lane = lax.rem(lax.broadcasted_iota(jnp.int32, (1, count), 1), each) < slots
    scale[...] = jnp.where(is_out, gate, 1.0)
    hit = lax.broadcasted_iota(jnp.int32, (block, count), 0) == pos
    put_out[...] = jnp.where(hit & is_out_lane, 1.0, 0.0).astype(BF)
    put_grad[...] = jnp.where(hit & ~is_out_lane, 1.0, 0.0).astype(BF)
    copies[0].wait()


def forward_body(*refs):
    *pieces, wg, wu, wd, part, part_sent = refs
    n = pieces[0].shape[0] // 2
    hid = wg.shape[2]
    xs = jnp.concatenate([piece[:n, :] for piece in pieces], axis=0)
    ys = jnp.concatenate([piece[n:, :] for piece in pieces], axis=0)
    for i, (rows, w) in enumerate(((xs, wg), (xs, wu), (ys, wd))):
        got = mm(rows, w[0])
        part[:, i * hid : (i + 1) * hid] = got
        part_sent[:, i * hid : (i + 1) * hid] = got.astype(BF)


def hold_body(src, dst):
    dst[...] = src[...]


def flip_body(*refs):
    for src, dst in zip(refs[:3], refs[3:]):
        dst[...] = src[0].T


def backward_body(n_pieces, n_recv, *refs):
    part, *rest = refs
    recv, rest = rest[:n_recv], rest[n_recv:]
    wg, wu, wd, rows_h, rows_a, rows_b, own, sib = rest
    hid = wg.shape[0]
    total = part[...]
    for other in recv:
        total = total + other[...].astype(F32)
    g, u, q = total[:, :hid], total[:, hid : 2 * hid], total[:, 2 * hid :]
    sig = jax.nn.sigmoid(g)
    h = (g * sig * u).astype(BF)
    a = (q * u * sig * (1.0 + g * (1.0 - sig))).astype(BF)
    b = (q * g * sig).astype(BF)
    rows_h[...] = h
    rows_a[...] = a
    rows_b[...] = b
    p = mm(h, wd[...]).astype(BF)
    e = (mm(a, wg[...]) + mm(b, wu[...])).astype(BF)
    n = part.shape[0] // n_pieces
    for i in range(n_pieces):
        out, at = (own, i) if 2 * i < n_pieces else (sib, i - n_pieces // 2)
        out[2 * at * n : (2 * at + 1) * n, :] = p[i * n : (i + 1) * n]
        out[(2 * at + 1) * n : (2 * at + 2) * n, :] = e[i * n : (i + 1) * n]


def pair_sum_body(own, got, *outs):
    n = own.shape[0] // len(outs)
    for j, out in enumerate(outs):
        at = slice(j * n, (j + 1) * n)
        out[...] = (own[at, :].astype(F32) + got[at, :].astype(F32)).astype(BF)


def return_body(n_dp, ks, slots, n_in, order, *refs):
    ins, outs = refs[:n_in], refs[n_in:]
    each = 2 * slots
    value = ins[0][...].astype(F32)
    for other in ins[1:]:
        value = value + other[...].astype(F32)
    pick = row_map(n_dp, ks, slots, lax.axis_index("dp"), False)
    rows = mm(pick, value.astype(BF)).astype(BF)
    for m, out in zip(order, outs):
        out[...] = rows[m * each : (m + 1) * each]


def home_body(n_dp, experts, order, put_out, put_grad, scale, *refs):
    msgs, outs, (layer_half, grad_half, wide, sems) = refs[:-6], refs[-6:-4], refs[-4:]
    msgs = dict(zip(order, msgs))
    batch = lax.axis_index("dp")
    each = msgs[0].shape[0]
    half = layer_half.shape[2]
    copies = []
    for dx in range(n_dp):
        for k in range(experts):
            wide[k * each : (k + 1) * each, :] = msgs[dx * experts + k][...].astype(F32)
        at = pl.ds(pl.multiple_of(lax.rem(batch + dx, n_dp) * half, 128), half)
        value = wide[...] * scale[...]
        high = value.astype(BF)
        low = (value - high.astype(F32)).astype(BF)
        grad_half[dx] = mm(put_grad[...], high).astype(BF)
        copies.append(pltpu.make_async_copy(grad_half.at[dx], outs[1].at[:, at], sems.at[2 * dx]))
        copies[-1].start()
        layer_half[dx] = (mm(put_out[...], high) + mm(put_out[...], low)).astype(BF)
        copies.append(
            pltpu.make_async_copy(layer_half.at[dx], outs[0].at[:, at], sems.at[2 * dx + 1])
        )
        copies[-1].start()
    for copy in copies:
        copy.wait()


def grads_body(*refs):
    pieces, lefts, (*outs, xs, ys, w, held, sems) = (
        refs[:SPLIT],
        refs[SPLIT : SPLIT + 6],
        refs[SPLIT + 6 :],
    )
    n = pieces[0].shape[0] // 2
    for i, piece in enumerate(pieces):
        xs[i * n : (i + 1) * n, :] = piece[:n, :]
        ys[i * n : (i + 1) * n, :] = piece[n:, :]
    copies = []
    for i, rows in enumerate((xs, xs, ys)):
        for j in range(2):
            left = lefts[3 * j + i]
            w[j * left.shape[0] : (j + 1) * left.shape[0], :] = left[...]
        held[i] = mm(rows[...], w[...], TN).astype(BF)
        copies.append(pltpu.make_async_copy(held.at[i], outs[i].at[0], sems.at[i]))
        copies[-1].start()
    for copy in copies:
        copy.wait()


def shards(n_dp, n_exp, tokens, routes, gate_values, wg, wu, wd, cot):
    block, width = tokens.shape
    experts = routes.shape[1]
    slots = routes.shape[2]
    hid = wg.shape[2]
    half = width // n_dp
    each = 2 * slots
    n_msg = n_dp * experts
    sds = jax.ShapeDtypeStruct

    def home_perm(dx, k, sign):
        return [
            (
                d * n_exp + i,
                (d + sign * dx) % n_dp * n_exp + (i // SPLIT + sign * k) % experts * SPLIT + i % SPLIT,
            )
            for d in range(n_dp)
            for i in range(n_exp)
        ]

    def part_perm(q):
        return [(d * n_exp + i, d * n_exp + (i ^ q)) for d in range(n_dp) for i in range(n_exp)]

    def batch_perm(dx):
        return [
            (d * n_exp + i, (d + dx) % n_dp * n_exp + i) for d in range(n_dp) for i in range(n_exp)
        ]

    def send(x, perm):
        return lax.ppermute(x, AXES, perm)

    kinds = [(dx, k) for dx in range(n_dp) for k in range(experts)]
    order = sorted(range(n_msg), key=lambda m: (kinds[m][1] == 0, kinds[m][0] == 0, m))
    small = [sds((each, half), BF)] * n_msg
    msgs = call(
        functools.partial(gather_body, n_dp, experts, slots),
        small,
        [in_hbm(x) for x in (routes[0], gate_values[0], tokens, cot)],
        in_specs=[HBM] * 4,
        scratch=[
            pltpu.VMEM((n_dp, 2 * block, half), BF),
            pltpu.SMEM((experts, slots), jnp.int32),
            pltpu.SMEM((experts, slots), F32),
            pltpu.SemaphoreType.DMA((2 + 2 * n_dp,)),
        ],
    )
    got = dict(zip(kinds, msgs))
    for kind in kinds[1:]:
        got[kind] = send(got[kind], home_perm(*kind, 1))
    count = each * experts
    small = [pltpu.SMEM((experts, slots), jnp.int32), pltpu.SMEM((experts, slots), F32)]
    down, put_out, put_grad, scale, mark = call(
        functools.partial(load_body, experts, slots),
        [sds(wd.shape, BF)] + [sds((block, count), BF)] * 2 + [sds((count, 1), F32)],
        [in_hbm(x) for x in (wd, routes[0], gate_values[0])],
        in_specs=[HBM] * 3,
        scratch=[*small, pltpu.SemaphoreType.DMA((3,))],
        mark=True,
    )
    rows = each * n_msg
    n_rows = rows // 2 * SPLIT
    (piece,) = call(
        functools.partial(arrange_body, n_dp, experts, slots, order),
        [sds((rows, half), BF)],
        [got[kinds[m]] for m in order],
        scratch=[pltpu.VMEM((rows, half), F32)],
        extra=rows * half * 8,
        after=[mark],
    )
    own_pieces = [piece] + [send(piece, part_perm(q)) for q in range(2, SPLIT, 2)]
    *flipped, last = call(
        flip_body, [sds((hid, half), BF)] * 3, (wg, wu, down), extra=8 * hid * half, mark=True
    )
    (own_pieces[-1],) = call(hold_body, [sds((rows, half), BF)], [own_pieces[-1]], after=[last])
    sib_pieces = [send(p, part_perm(1)) for p in own_pieces]
    chips = SPLIT // 2
    halves = [(0, chips - 1), tuple(range(1, chips - 1))]
    ordered = [[own_pieces[j] for j in js] + [sib_pieces[j] for j in js] for js in halves]
    mark, parts, recv = (), [], []
    for i, pieces in enumerate(ordered):
        n = len(pieces) * rows // 2
        part, part_sent, *mark = call(
            forward_body,
            [sds((n, 3 * hid), F32), sds((n, 3 * hid), BF)],
            (*pieces, wg, wu, down),
            extra=2 * n * half * 2 + n * hid * 4,
            after=mark,
            mark=i == 0,
        )
        parts.append(part)
        recv.append([send(part_sent, batch_perm(dx)) for dx in range(1, n_dp)])
    lefts, sums, mark = [], {}, ()
    for i, js in enumerate(halves):
        n = parts[i].shape[0]
        rows_h, rows_a, rows_b, own, sib, *mark = call(
            functools.partial(backward_body, 2 * len(js), n_dp - 1),
            [sds((n, hid), BF)] * 3 + [sds((n, half), BF)] * 2,
            (parts[i], *recv[i], *flipped),
            extra=n * half * 12,
            after=mark,
            mark=i == 0,
        )
        lefts += [rows_a, rows_b, rows_h]
        got = call(
            pair_sum_body, [sds((rows, half), BF)] * len(js), (own, send(sib, part_perm(1)))
        )
        sums.update(zip(js, got))
    back = [sums[0]] + [send(sums[j], part_perm(2 * j)) for js in halves for j in js if j]
    *grads, mark = call(
        grads_body,
        [sds((1, half, hid), BF)] * 3,
        (*ordered[0], *ordered[1], *lefts),
        out_specs=[HBM] * 3,
        scratch=[pltpu.VMEM((n_rows, half), BF)] * 2
        + [
            pltpu.VMEM((n_rows, hid), BF),
            pltpu.VMEM((3, half, hid), BF),
            pltpu.SemaphoreType.DMA((3,)),
        ],
        extra=n_rows * half * 8 + half * hid * 12,
        mark=True,
        cost=pl.CostEstimate(
            flops=6 * n_rows * half * hid, bytes_accessed=6 * half * hid, transcendentals=0
        ),
    )
    msgs = call(
        functools.partial(return_body, n_dp, experts, slots, len(back), order),
        [sds((each, half), BF)] * n_msg,
        back,
        extra=rows * half * 8,
        after=[mark],
    )
    got = {kinds[m]: msg for m, msg in zip(order, msgs)}
    for kind in kinds[1:]:
        got[kind] = send(got[kind], home_perm(*kind, -1))
    layer_out, token_grad = call(
        functools.partial(home_body, n_dp, experts, order),
        [sds((block, width), BF)] * 2,
        (put_out, put_grad, scale, *[got[kinds[m]] for m in order]),
        out_specs=[HBM] * 2,
        scratch=[pltpu.VMEM((n_dp, block, half), BF)] * 2
        + [pltpu.VMEM((count, half), F32), pltpu.SemaphoreType.DMA((2 * n_dp,))],
        extra=block * half * 16 + count * half * 4,
    )
    return layer_out, token_grad, *grads


def solution(mesh):
    rows = P(AXES, None)
    slots = P(AXES, None, None)
    weights = P("expert", "dp", None)
    return jax.shard_map(
        functools.partial(shards, mesh.shape["dp"], mesh.shape["expert"]),
        mesh=mesh,
        in_specs=(rows, slots, slots, weights, weights, weights, rows),
        out_specs=(rows, rows, weights, weights, weights),
        check_vma=False,
    )
```

```python
import functools
import math

import jax
import jax.numpy as jnp
from jax import lax
from jax.experimental import pallas as pl
from jax.experimental.pallas import tpu as pltpu
from jax.sharding import PartitionSpec as P

SPLIT = 8
BF = jnp.bfloat16
F32 = jnp.float32
AXES = ("dp", "expert")
TN = (((0,), (0,)), ((), ()))
ANY = pl.BlockSpec(memory_space=pl.ANY)
HBM = pl.BlockSpec(memory_space=pltpu.HBM)
VMEM = pl.BlockSpec(memory_space=pltpu.VMEM)


def mm(a, b, dims=None):
    if dims is None:
        return jnp.dot(a, b, preferred_element_type=F32)
    return lax.dot_general(a, b, dims, preferred_element_type=F32)


def in_hbm(x):
    return pltpu.with_memory_space_constraint(x, pltpu.HBM)


def size(x):
    return math.prod(x.shape) * jnp.dtype(x.dtype).itemsize


def call(
    body,
    out_shape,
    args,
    in_specs=None,
    out_specs=None,
    scratch=(),
    extra=0,
    after=(),
    mark=False,
    cost=None,
):
    n_in, n_out = len(args), len(out_shape)
    used = sum(map(size, args)) + sum(map(size, out_shape)) + extra
    in_specs = in_specs or [VMEM] * n_in
    out_specs = out_specs or [VMEM] * n_out

    def whole(*refs):
        ins, rest = refs[:n_in], refs[n_in + len(after) :]
        outs, rest = rest[:n_out], rest[n_out:]
        if mark:
            rest[0][...] = jnp.zeros_like(rest[0])
            rest = rest[1:]
        body(*ins, *outs, *rest)

    return pl.pallas_call(
        whole,
        out_shape=[*out_shape, *[jax.ShapeDtypeStruct((8, 128), F32)] * mark],
        in_specs=[*in_specs, *[ANY] * len(after)],
        out_specs=[*out_specs, *[VMEM] * mark],
        scratch_shapes=list(scratch),
        compiler_params=pltpu.CompilerParams(vmem_limit_bytes=min(2 * used + (4 << 20), 56 << 20)),
        cost_estimate=cost,
    )(*args, *after)


def slot_values(read, count, slots, expert, experts, axis):
    shape = (count, 1) if axis == 0 else (1, count)
    place = lax.broadcasted_iota(jnp.int32, shape, axis)
    value = None
    for k in range(experts):
        e = lax.rem(expert + k, experts)
        for j in range(2 * slots):
            here = read(e, j % slots)
            if value is None:
                value = jnp.full(shape, here)
            else:
                value = jnp.where(place == k * 2 * slots + j, here, value)
    return value


def own_expert(experts):
    return lax.div(lax.axis_index("expert"), SPLIT)


def gather_body(n_dp, experts, slots, routes_in, gates_in, tokens, cot, *refs):
    *outs, both, routes, gates, sems = refs
    batch = lax.axis_index("dp")
    expert = own_expert(experts)
    count = 2 * slots * experts
    block = tokens.shape[0]
    half = tokens.shape[1] // n_dp
    moves = [(routes_in, routes), (gates_in, gates)]
    for dx in range(n_dp):
        at = pl.ds(pl.multiple_of(lax.rem(batch + dx, n_dp) * half, 128), half)
        for i, src in enumerate((tokens, cot)):
            moves.append((src.at[:, at], both.at[dx, pl.ds(i * block, block)]))
    copies = [pltpu.make_async_copy(*move, sems.at[i]) for i, move in enumerate(moves)]
    for copy in copies:
        copy.start()
    for copy in copies[:2]:
        copy.wait()
    pos = slot_values(lambda e, s: routes[e, s], count, slots, expert, experts, 0)
    gate = slot_values(lambda e, s: gates[e, s], count, slots, expert, experts, 0)
    is_token = lax.rem(lax.broadcasted_iota(jnp.int32, (count, 1), 0), 2 * slots) < slots
    scale = jnp.where(is_token, 1.0, gate)
    row = jnp.where(is_token, pos, pos + block)
    hit = lax.broadcasted_iota(jnp.int32, (count, 2 * block), 1) == row
    pick = jnp.where(hit, 1.0, 0.0).astype(BF)
    for dx in range(n_dp):
        for copy in copies[2 + 2 * dx : 4 + 2 * dx]:
            copy.wait()
        rows = (mm(pick, both[dx]) * scale).astype(BF)
        for k in range(experts):
            outs[dx * experts + k][...] = rows[k * 2 * slots : (k + 1) * 2 * slots]


def row_map(n_dp, ks, slots, batch, to_block):
    each = 2 * slots
    total = each * n_dp * ks
    r = lax.broadcasted_iota(jnp.int32, (total, 1), 0)
    if to_block:
        kind, rest = lax.div(r, total // 2), lax.rem(r, total // 2)
        b, rest = lax.div(rest, ks * slots), lax.rem(rest, ks * slots)
        k, s = lax.div(rest, slots), lax.rem(rest, slots)
        dx = lax.rem(batch - b + n_dp, n_dp)
        source = (dx * ks + k) * each + kind * slots + s
    else:
        m, j = lax.div(r, each), lax.rem(r, each)
        dx, k = lax.div(m, ks), lax.rem(m, ks)
        kind, s = lax.div(j, slots), lax.rem(j, slots)
        b = lax.rem(batch - dx + n_dp, n_dp)
        source = kind * (total // 2) + (b * ks + k) * slots + s
    pick = lax.broadcasted_iota(jnp.int32, (total, total), 1) == source
    return jnp.where(pick, 1.0, 0.0).astype(BF)


def arrange_body(n_dp, experts, slots, order, *refs):
    *msgs, out, wide = refs
    each = 2 * slots
    for m, msg in zip(order, msgs):
        wide[m * each : (m + 1) * each, :] = msg[...].astype(F32)
    pick = row_map(n_dp, experts, slots, lax.axis_index("dp"), True)
    out[...] = mm(pick, wide[...].astype(BF)).astype(BF)


def load_body(experts, slots, src, routes_in, gates_in, dst, put_out, put_grad, scale, routes, gates, sems):
    moves = ((src, dst), (routes_in, routes), (gates_in, gates))
    copies = [pltpu.make_async_copy(*move, sems.at[i]) for i, move in enumerate(moves)]
    for copy in copies:
        copy.start()
    for copy in copies[1:]:
        copy.wait()
    expert = own_expert(experts)
    each = 2 * slots
    count = each * experts
    block = put_out.shape[0]
    pos = slot_values(lambda e, s: routes[e, s], count, slots, expert, experts, 1)
    gate = slot_values(lambda e, s: gates[e, s], count, slots, expert, experts, 0)
    is_out = lax.rem(lax.broadcasted_iota(jnp.int32, (count, 1), 0), each) < slots
    is_out_lane = lax.rem(lax.broadcasted_iota(jnp.int32, (1, count), 1), each) < slots
    scale[...] = jnp.where(is_out, gate, 1.0)
    hit = lax.broadcasted_iota(jnp.int32, (block, count), 0) == pos
    put_out[...] = jnp.where(hit & is_out_lane, 1.0, 0.0).astype(BF)
    put_grad[...] = jnp.where(hit & ~is_out_lane, 1.0, 0.0).astype(BF)
    copies[0].wait()


def forward_body(*refs):
    *pieces, wg, wu, wd, part, part_sent = refs
    n = pieces[0].shape[0] // 2
    hid = wg.shape[2]
    xs = jnp.concatenate([piece[:n, :] for piece in pieces], axis=0)
    ys = jnp.concatenate([piece[n:, :] for piece in pieces], axis=0)
    for i, (rows, w) in enumerate(((xs, wg), (xs, wu), (ys, wd))):
        got = mm(rows, w[0])
        part[:, i * hid : (i + 1) * hid] = got
        part_sent[:, i * hid : (i + 1) * hid] = got.astype(BF)


def hold_body(src, dst):
    dst[...] = src[...]


def flip_body(*refs):
    for src, dst in zip(refs[:3], refs[3:]):
        dst[...] = src[0].T


def backward_body(n_pieces, n_recv, *refs):
    part, *rest = refs
    recv, rest = rest[:n_recv], rest[n_recv:]
    wg, wu, wd, rows_h, rows_a, rows_b, own, sib = rest
    hid = wg.shape[0]
    total = part[...]
    for other in recv:
        total = total + other[...].astype(F32)
    g, u, q = total[:, :hid], total[:, hid : 2 * hid], total[:, 2 * hid :]
    sig = jax.nn.sigmoid(g)
    h = (g * sig * u).astype(BF)
    a = (q * u * sig * (1.0 + g * (1.0 - sig))).astype(BF)
    b = (q * g * sig).astype(BF)
    rows_h[...] = h
    rows_a[...] = a
    rows_b[...] = b
    p = mm(h, wd[...]).astype(BF)
    e = (mm(a, wg[...]) + mm(b, wu[...])).astype(BF)
    n = part.shape[0] // n_pieces
    for i in range(n_pieces):
        out, at = (own, i) if 2 * i < n_pieces else (sib, i - n_pieces // 2)
        out[2 * at * n : (2 * at + 1) * n, :] = p[i * n : (i + 1) * n]
        out[(2 * at + 1) * n : (2 * at + 2) * n, :] = e[i * n : (i + 1) * n]


def pair_sum_body(own, got, *outs):
    n = own.shape[0] // len(outs)
    for j, out in enumerate(outs):
        at = slice(j * n, (j + 1) * n)
        out[...] = (own[at, :].astype(F32) + got[at, :].astype(F32)).astype(BF)


def return_body(n_dp, ks, slots, n_in, order, *refs):
    ins, outs = refs[:n_in], refs[n_in:]
    each = 2 * slots
    value = ins[0][...].astype(F32)
    for other in ins[1:]:
        value = value + other[...].astype(F32)
    pick = row_map(n_dp, ks, slots, lax.axis_index("dp"), False)
    rows = mm(pick, value.astype(BF)).astype(BF)
    for m, out in zip(order, outs):
        out[...] = rows[m * each : (m + 1) * each]


def home_body(n_dp, experts, order, parts, put_out, put_grad, scale, *refs):
    msgs, outs, (layer_half, grad_half, wide, sems) = refs[:-6], refs[-6:-4], refs[-4:]
    msgs = dict(zip(order, msgs))
    batch = lax.axis_index("dp")
    each = msgs[0].shape[0]
    half = layer_half.shape[2]
    step = half // parts
    put_out, put_grad, scale = put_out[...], put_grad[...], scale[...]
    put_both = jnp.concatenate([put_out, put_out], axis=1)
    copies = []
    for dx in range(n_dp):
        for k in range(experts):
            wide[k * each : (k + 1) * each, :] = msgs[dx * experts + k][...].astype(F32)
        first = lax.rem(batch + dx, n_dp) * half
        for c in range(parts):
            at = slice(c * step, (c + 1) * step)
            value = wide[:, at] * scale
            high = value.astype(BF)
            low = (value - high.astype(F32)).astype(BF)
            grad_half[dx, :, at] = mm(put_grad, high).astype(BF)
            layer_half[dx, :, at] = mm(put_both, jnp.concatenate([high, low], axis=0)).astype(BF)
            to = pl.ds(pl.multiple_of(first + c * step, 128), step)
            for src, dst in ((grad_half, outs[1]), (layer_half, outs[0])):
                copy = pltpu.make_async_copy(
                    src.at[dx, :, pl.ds(c * step, step)], dst.at[:, to], sems.at[len(copies)]
                )
                copy.start()
                copies.append(copy)
    for copy in copies:
        copy.wait()


def grads_body(*refs):
    pieces, lefts, (*outs, xs, ys, w, held, sems) = (
        refs[:SPLIT],
        refs[SPLIT : SPLIT + 6],
        refs[SPLIT + 6 :],
    )
    n = pieces[0].shape[0] // 2
    for i, piece in enumerate(pieces):
        xs[i * n : (i + 1) * n, :] = piece[:n, :]
        ys[i * n : (i + 1) * n, :] = piece[n:, :]
    copies = []
    for i, rows in enumerate((xs, xs, ys)):
        for j in range(2):
            left = lefts[3 * j + i]
            w[j * left.shape[0] : (j + 1) * left.shape[0], :] = left[...]
        held[i] = mm(rows[...], w[...], TN).astype(BF)
        copies.append(pltpu.make_async_copy(held.at[i], outs[i].at[0], sems.at[i]))
        copies[-1].start()
    for copy in copies:
        copy.wait()


def shards(n_dp, n_exp, tokens, routes, gate_values, wg, wu, wd, cot):
    block, width = tokens.shape
    experts = routes.shape[1]
    slots = routes.shape[2]
    hid = wg.shape[2]
    half = width // n_dp
    each = 2 * slots
    n_msg = n_dp * experts
    sds = jax.ShapeDtypeStruct

    def home_perm(dx, k, sign):
        return [
            (
                d * n_exp + i,
                (d + sign * dx) % n_dp * n_exp + (i // SPLIT + sign * k) % experts * SPLIT + i % SPLIT,
            )
            for d in range(n_dp)
            for i in range(n_exp)
        ]

    def part_perm(q):
        return [(d * n_exp + i, d * n_exp + (i ^ q)) for d in range(n_dp) for i in range(n_exp)]

    def batch_perm(dx):
        return [
            (d * n_exp + i, (d + dx) % n_dp * n_exp + i) for d in range(n_dp) for i in range(n_exp)
        ]

    def send(x, perm):
        return lax.ppermute(x, AXES, perm)

    kinds = [(dx, k) for dx in range(n_dp) for k in range(experts)]
    order = sorted(range(n_msg), key=lambda m: (kinds[m][1] == 0, kinds[m][0] == 0, m))
    small = [sds((each, half), BF)] * n_msg
    msgs = call(
        functools.partial(gather_body, n_dp, experts, slots),
        small,
        [in_hbm(x) for x in (routes[0], gate_values[0], tokens, cot)],
        in_specs=[HBM] * 4,
        scratch=[
            pltpu.VMEM((n_dp, 2 * block, half), BF),
            pltpu.SMEM((experts, slots), jnp.int32),
            pltpu.SMEM((experts, slots), F32),
            pltpu.SemaphoreType.DMA((2 + 2 * n_dp,)),
        ],
    )
    got = dict(zip(kinds, msgs))
    for kind in kinds[1:]:
        got[kind] = send(got[kind], home_perm(*kind, 1))
    count = each * experts
    small = [pltpu.SMEM((experts, slots), jnp.int32), pltpu.SMEM((experts, slots), F32)]
    down, put_out, put_grad, scale, mark = call(
        functools.partial(load_body, experts, slots),
        [sds(wd.shape, BF)] + [sds((block, count), BF)] * 2 + [sds((count, 1), F32)],
        [in_hbm(x) for x in (wd, routes[0], gate_values[0])],
        in_specs=[HBM] * 3,
        scratch=[*small, pltpu.SemaphoreType.DMA((3,))],
        mark=True,
    )
    rows = each * n_msg
    n_rows = rows // 2 * SPLIT
    (piece,) = call(
        functools.partial(arrange_body, n_dp, experts, slots, order),
        [sds((rows, half), BF)],
        [got[kinds[m]] for m in order],
        scratch=[pltpu.VMEM((rows, half), F32)],
        extra=rows * half * 8,
        after=[mark],
    )
    own_pieces = [piece] + [send(piece, part_perm(q)) for q in range(2, SPLIT, 2)]
    *flipped, last = call(
        flip_body, [sds((hid, half), BF)] * 3, (wg, wu, down), extra=8 * hid * half, mark=True
    )
    (own_pieces[-1],) = call(hold_body, [sds((rows, half), BF)], [own_pieces[-1]], after=[last])
    sib_pieces = [send(p, part_perm(1)) for p in own_pieces]
    chips = SPLIT // 2
    halves = [(0, chips - 1), tuple(range(1, chips - 1))]
    ordered = [[own_pieces[j] for j in js] + [sib_pieces[j] for j in js] for js in halves]
    mark, parts, recv = (), [], []
    for i, pieces in enumerate(ordered):
        n = len(pieces) * rows // 2
        part, part_sent, *mark = call(
            forward_body,
            [sds((n, 3 * hid), F32), sds((n, 3 * hid), BF)],
            (*pieces, wg, wu, down),
            extra=2 * n * half * 2 + n * hid * 4,
            after=mark,
            mark=i == 0,
        )
        parts.append(part)
        recv.append([send(part_sent, batch_perm(dx)) for dx in range(1, n_dp)])
    lefts, sums, mark = [], {}, ()
    for i, js in enumerate(halves):
        n = parts[i].shape[0]
        rows_h, rows_a, rows_b, own, sib, *mark = call(
            functools.partial(backward_body, 2 * len(js), n_dp - 1),
            [sds((n, hid), BF)] * 3 + [sds((n, half), BF)] * 2,
            (parts[i], *recv[i], *flipped),
            extra=n * half * 12,
            after=mark,
            mark=i == 0,
        )
        lefts += [rows_a, rows_b, rows_h]
        got = call(
            pair_sum_body, [sds((rows, half), BF)] * len(js), (own, send(sib, part_perm(1)))
        )
        sums.update(zip(js, got))
    back = [sums[0]] + [send(sums[j], part_perm(2 * j)) for js in halves for j in js if j]
    *grads, mark = call(
        grads_body,
        [sds((1, half, hid), BF)] * 3,
        (*ordered[0], *ordered[1], *lefts),
        out_specs=[HBM] * 3,
        scratch=[pltpu.VMEM((n_rows, half), BF)] * 2
        + [
            pltpu.VMEM((n_rows, hid), BF),
            pltpu.VMEM((3, half, hid), BF),
            pltpu.SemaphoreType.DMA((3,)),
        ],
        extra=n_rows * half * 8 + half * hid * 12,
        mark=True,
        cost=pl.CostEstimate(
            flops=6 * n_rows * half * hid, bytes_accessed=6 * half * hid, transcendentals=0
        ),
    )
    msgs = call(
        functools.partial(return_body, n_dp, experts, slots, len(back), order),
        [sds((each, half), BF)] * n_msg,
        back,
        extra=rows * half * 8,
        after=[mark],
    )
    got = {kinds[m]: msg for m, msg in zip(order, msgs)}
    for kind in kinds[1:]:
        got[kind] = send(got[kind], home_perm(*kind, -1))
    parts = 2
    layer_out, token_grad = call(
        functools.partial(home_body, n_dp, experts, order, parts),
        [sds((block, width), BF)] * 2,
        (put_out, put_grad, scale, *[got[kinds[m]] for m in order]),
        out_specs=[HBM] * 2,
        scratch=[pltpu.VMEM((n_dp, block, half), BF)] * 2
        + [pltpu.VMEM((count, half), F32), pltpu.SemaphoreType.DMA((2 * n_dp * parts,))],
        extra=block * half * 16 + count * half * 4,
    )
    return layer_out, token_grad, *grads


def solution(mesh):
    rows = P(AXES, None)
    slots = P(AXES, None, None)
    weights = P("expert", "dp", None)
    return jax.shard_map(
        functools.partial(shards, mesh.shape["dp"], mesh.shape["expert"]),
        mesh=mesh,
        in_specs=(rows, slots, slots, weights, weights, weights, rows),
        out_specs=(rows, rows, weights, weights, weights),
        check_vma=False,
    )
```

```python
import functools
import math

import jax
import jax.numpy as jnp
from jax import lax
from jax.experimental import pallas as pl
from jax.experimental.pallas import tpu as pltpu
from jax.sharding import PartitionSpec as P

SPLIT = 8
BF = jnp.bfloat16
F32 = jnp.float32
AXES = ("dp", "expert")
TN = (((0,), (0,)), ((), ()))
ANY = pl.BlockSpec(memory_space=pl.ANY)
HBM = pl.BlockSpec(memory_space=pltpu.HBM)
VMEM = pl.BlockSpec(memory_space=pltpu.VMEM)


def mm(a, b, dims=None):
    if dims is None:
        return jnp.dot(a, b, preferred_element_type=F32)
    return lax.dot_general(a, b, dims, preferred_element_type=F32)


def in_hbm(x):
    return pltpu.with_memory_space_constraint(x, pltpu.HBM)


def size(x):
    return math.prod(x.shape) * jnp.dtype(x.dtype).itemsize


def call(
    body,
    out_shape,
    args,
    in_specs=None,
    out_specs=None,
    scratch=(),
    extra=0,
    after=(),
    mark=False,
    cost=None,
):
    n_in, n_out = len(args), len(out_shape)
    used = sum(map(size, args)) + sum(map(size, out_shape)) + extra
    in_specs = in_specs or [VMEM] * n_in
    out_specs = out_specs or [VMEM] * n_out

    def whole(*refs):
        ins, rest = refs[:n_in], refs[n_in + len(after) :]
        outs, rest = rest[:n_out], rest[n_out:]
        if mark:
            rest[0][...] = jnp.zeros_like(rest[0])
            rest = rest[1:]
        body(*ins, *outs, *rest)

    return pl.pallas_call(
        whole,
        out_shape=[*out_shape, *[jax.ShapeDtypeStruct((8, 128), F32)] * mark],
        in_specs=[*in_specs, *[ANY] * len(after)],
        out_specs=[*out_specs, *[VMEM] * mark],
        scratch_shapes=list(scratch),
        compiler_params=pltpu.CompilerParams(vmem_limit_bytes=min(2 * used + (4 << 20), 56 << 20)),
        cost_estimate=cost,
    )(*args, *after)


def slot_values(read, count, slots, expert, experts, axis):
    shape = (count, 1) if axis == 0 else (1, count)
    place = lax.broadcasted_iota(jnp.int32, shape, axis)
    value = None
    for k in range(experts):
        e = lax.rem(expert + k, experts)
        for j in range(2 * slots):
            here = read(e, j % slots)
            if value is None:
                value = jnp.full(shape, here)
            else:
                value = jnp.where(place == k * 2 * slots + j, here, value)
    return value


def own_expert(experts):
    return lax.div(lax.axis_index("expert"), SPLIT)


def gather_body(n_dp, experts, slots, routes_in, gates_in, tokens, cot, *refs):
    *outs, both, routes, gates, sems = refs
    batch = lax.axis_index("dp")
    expert = own_expert(experts)
    count = 2 * slots * experts
    block = tokens.shape[0]
    half = tokens.shape[1] // n_dp
    moves = [(routes_in, routes), (gates_in, gates)]
    for dx in range(n_dp):
        at = pl.ds(pl.multiple_of(lax.rem(batch + dx, n_dp) * half, 128), half)
        for i, src in enumerate((tokens, cot)):
            moves.append((src.at[:, at], both.at[dx, pl.ds(i * block, block)]))
    copies = [pltpu.make_async_copy(*move, sems.at[i]) for i, move in enumerate(moves)]
    for copy in copies:
        copy.start()
    for copy in copies[:2]:
        copy.wait()
    pos = slot_values(lambda e, s: routes[e, s], count, slots, expert, experts, 0)
    gate = slot_values(lambda e, s: gates[e, s], count, slots, expert, experts, 0)
    is_token = lax.rem(lax.broadcasted_iota(jnp.int32, (count, 1), 0), 2 * slots) < slots
    scale = jnp.where(is_token, 1.0, gate)
    row = jnp.where(is_token, pos, pos + block)
    hit = lax.broadcasted_iota(jnp.int32, (count, 2 * block), 1) == row
    pick = jnp.where(hit, 1.0, 0.0).astype(BF)
    for dx in range(n_dp):
        for copy in copies[2 + 2 * dx : 4 + 2 * dx]:
            copy.wait()
        rows = (mm(pick, both[dx]) * scale).astype(BF)
        for k in range(experts):
            outs[dx * experts + k][...] = rows[k * 2 * slots : (k + 1) * 2 * slots]


def row_map(n_dp, ks, slots, batch, to_block):
    each = 2 * slots
    total = each * n_dp * ks
    r = lax.broadcasted_iota(jnp.int32, (total, 1), 0)
    if to_block:
        kind, rest = lax.div(r, total // 2), lax.rem(r, total // 2)
        b, rest = lax.div(rest, ks * slots), lax.rem(rest, ks * slots)
        k, s = lax.div(rest, slots), lax.rem(rest, slots)
        dx = lax.rem(batch - b + n_dp, n_dp)
        source = (dx * ks + k) * each + kind * slots + s
    else:
        m, j = lax.div(r, each), lax.rem(r, each)
        dx, k = lax.div(m, ks), lax.rem(m, ks)
        kind, s = lax.div(j, slots), lax.rem(j, slots)
        b = lax.rem(batch - dx + n_dp, n_dp)
        source = kind * (total // 2) + (b * ks + k) * slots + s
    pick = lax.broadcasted_iota(jnp.int32, (total, total), 1) == source
    return jnp.where(pick, 1.0, 0.0).astype(BF)


def arrange_body(n_dp, experts, slots, order, *refs):
    *msgs, out, wide = refs
    each = 2 * slots
    for m, msg in zip(order, msgs):
        wide[m * each : (m + 1) * each, :] = msg[...].astype(F32)
    pick = row_map(n_dp, experts, slots, lax.axis_index("dp"), True)
    out[...] = mm(pick, wide[...].astype(BF)).astype(BF)


def load_body(experts, slots, src, routes_in, gates_in, dst, put_out, put_grad, scale, routes, gates, sems):
    moves = ((src, dst), (routes_in, routes), (gates_in, gates))
    copies = [pltpu.make_async_copy(*move, sems.at[i]) for i, move in enumerate(moves)]
    for copy in copies:
        copy.start()
    for copy in copies[1:]:
        copy.wait()
    expert = own_expert(experts)
    each = 2 * slots
    count = each * experts
    block = put_out.shape[0]
    pos = slot_values(lambda e, s: routes[e, s], count, slots, expert, experts, 1)
    gate = slot_values(lambda e, s: gates[e, s], count, slots, expert, experts, 0)
    is_out = lax.rem(lax.broadcasted_iota(jnp.int32, (count, 1), 0), each) < slots
    is_out_lane = lax.rem(lax.broadcasted_iota(jnp.int32, (1, count), 1), each) < slots
    scale[...] = jnp.where(is_out, gate, 1.0)
    hit = lax.broadcasted_iota(jnp.int32, (block, count), 0) == pos
    put_out[...] = jnp.where(hit & is_out_lane, 1.0, 0.0).astype(BF)
    put_grad[...] = jnp.where(hit & ~is_out_lane, 1.0, 0.0).astype(BF)
    copies[0].wait()


def forward_body(*refs):
    *pieces, wg, wu, wd, part, part_sent = refs
    n = pieces[0].shape[0] // 2
    hid = wg.shape[2]
    xs = jnp.concatenate([piece[:n, :] for piece in pieces], axis=0)
    ys = jnp.concatenate([piece[n:, :] for piece in pieces], axis=0)
    for i, (rows, w) in enumerate(((xs, wg), (xs, wu), (ys, wd))):
        got = mm(rows, w[0])
        part[:, i * hid : (i + 1) * hid] = got
        part_sent[:, i * hid : (i + 1) * hid] = got.astype(BF)


def hold_body(src, dst):
    dst[...] = src[...]


def flip_body(wg_in, wu_in, wd, wg, wu, wg_t, wu_t, wd_t, sems):
    copies = [
        pltpu.make_async_copy(src, dst, sems.at[i])
        for i, (src, dst) in enumerate(((wg_in, wg), (wu_in, wu)))
    ]
    for copy in copies:
        copy.start()
    wd_t[...] = wd[0].T
    for copy, src, dst in zip(copies, (wg, wu), (wg_t, wu_t)):
        copy.wait()
        dst[...] = src[0].T


def backward_body(n_pieces, n_recv, *refs):
    part, *rest = refs
    recv, rest = rest[:n_recv], rest[n_recv:]
    wg, wu, wd, rows_h, rows_a, rows_b, own, sib = rest
    hid = wg.shape[0]
    total = part[...]
    for other in recv:
        total = total + other[...].astype(F32)
    g, u, q = total[:, :hid], total[:, hid : 2 * hid], total[:, 2 * hid :]
    sig = jax.nn.sigmoid(g)
    h = (g * sig * u).astype(BF)
    a = (q * u * sig * (1.0 + g * (1.0 - sig))).astype(BF)
    b = (q * g * sig).astype(BF)
    rows_h[...] = h
    rows_a[...] = a
    rows_b[...] = b
    p = mm(h, wd[...]).astype(BF)
    e = (mm(a, wg[...]) + mm(b, wu[...])).astype(BF)
    n = part.shape[0] // n_pieces
    for i in range(n_pieces):
        out, at = (own, i) if 2 * i < n_pieces else (sib, i - n_pieces // 2)
        out[2 * at * n : (2 * at + 1) * n, :] = p[i * n : (i + 1) * n]
        out[(2 * at + 1) * n : (2 * at + 2) * n, :] = e[i * n : (i + 1) * n]


def pair_sum_body(own, got, *outs):
    n = own.shape[0] // len(outs)
    for j, out in enumerate(outs):
        at = slice(j * n, (j + 1) * n)
        out[...] = (own[at, :].astype(F32) + got[at, :].astype(F32)).astype(BF)


def return_body(n_dp, ks, slots, n_in, order, *refs):
    ins, outs = refs[:n_in], refs[n_in:]
    each = 2 * slots
    value = ins[0][...].astype(F32)
    for other in ins[1:]:
        value = value + other[...].astype(F32)
    pick = row_map(n_dp, ks, slots, lax.axis_index("dp"), False)
    rows = mm(pick, value.astype(BF)).astype(BF)
    for m, out in zip(order, outs):
        out[...] = rows[m * each : (m + 1) * each]


def home_body(n_dp, experts, order, parts, put_out, put_grad, scale, *refs):
    msgs, outs, (layer_half, grad_half, wide, sems) = refs[:-6], refs[-6:-4], refs[-4:]
    msgs = dict(zip(order, msgs))
    batch = lax.axis_index("dp")
    each = msgs[0].shape[0]
    half = layer_half.shape[2]
    step = half // parts
    put_out, put_grad, scale = put_out[...], put_grad[...], scale[...]
    put_both = jnp.concatenate([put_out, put_out], axis=1)
    copies = []
    for dx in range(n_dp):
        for k in range(experts):
            wide[k * each : (k + 1) * each, :] = msgs[dx * experts + k][...].astype(F32)
        first = lax.rem(batch + dx, n_dp) * half
        for c in range(parts):
            at = slice(c * step, (c + 1) * step)
            value = wide[:, at] * scale
            high = value.astype(BF)
            low = (value - high.astype(F32)).astype(BF)
            grad_half[dx, :, at] = mm(put_grad, high).astype(BF)
            layer_half[dx, :, at] = mm(put_both, jnp.concatenate([high, low], axis=0)).astype(BF)
            to = pl.ds(pl.multiple_of(first + c * step, 128), step)
            for src, dst in ((grad_half, outs[1]), (layer_half, outs[0])):
                copy = pltpu.make_async_copy(
                    src.at[dx, :, pl.ds(c * step, step)], dst.at[:, to], sems.at[len(copies)]
                )
                copy.start()
                copies.append(copy)
    for copy in copies:
        copy.wait()


def grads_body(*refs):
    pieces, lefts, (*outs, xs, ys, w, held, sems) = (
        refs[:SPLIT],
        refs[SPLIT : SPLIT + 6],
        refs[SPLIT + 6 :],
    )
    n = pieces[0].shape[0] // 2
    for i, piece in enumerate(pieces):
        xs[i * n : (i + 1) * n, :] = piece[:n, :]
        ys[i * n : (i + 1) * n, :] = piece[n:, :]
    copies = []
    for i, rows in enumerate((xs, xs, ys)):
        for j in range(2):
            left = lefts[3 * j + i]
            w[j * left.shape[0] : (j + 1) * left.shape[0], :] = left[...]
        held[i] = mm(rows[...], w[...], TN).astype(BF)
        copies.append(pltpu.make_async_copy(held.at[i], outs[i].at[0], sems.at[i]))
        copies[-1].start()
    for copy in copies:
        copy.wait()


def shards(n_dp, n_exp, tokens, routes, gate_values, wg, wu, wd, cot):
    block, width = tokens.shape
    experts = routes.shape[1]
    slots = routes.shape[2]
    hid = wg.shape[2]
    half = width // n_dp
    each = 2 * slots
    n_msg = n_dp * experts
    sds = jax.ShapeDtypeStruct

    def home_perm(dx, k, sign):
        return [
            (
                d * n_exp + i,
                (d + sign * dx) % n_dp * n_exp + (i // SPLIT + sign * k) % experts * SPLIT + i % SPLIT,
            )
            for d in range(n_dp)
            for i in range(n_exp)
        ]

    def part_perm(q):
        return [(d * n_exp + i, d * n_exp + (i ^ q)) for d in range(n_dp) for i in range(n_exp)]

    def batch_perm(dx):
        return [
            (d * n_exp + i, (d + dx) % n_dp * n_exp + i) for d in range(n_dp) for i in range(n_exp)
        ]

    def send(x, perm):
        return lax.ppermute(x, AXES, perm)

    kinds = [(dx, k) for dx in range(n_dp) for k in range(experts)]
    order = sorted(range(n_msg), key=lambda m: (kinds[m][1] == 0, kinds[m][0] == 0, m))
    small = [sds((each, half), BF)] * n_msg
    msgs = call(
        functools.partial(gather_body, n_dp, experts, slots),
        small,
        [in_hbm(x) for x in (routes[0], gate_values[0], tokens, cot)],
        in_specs=[HBM] * 4,
        scratch=[
            pltpu.VMEM((n_dp, 2 * block, half), BF),
            pltpu.SMEM((experts, slots), jnp.int32),
            pltpu.SMEM((experts, slots), F32),
            pltpu.SemaphoreType.DMA((2 + 2 * n_dp,)),
        ],
    )
    got = dict(zip(kinds, msgs))
    for kind in kinds[1:]:
        got[kind] = send(got[kind], home_perm(*kind, 1))
    count = each * experts
    small = [pltpu.SMEM((experts, slots), jnp.int32), pltpu.SMEM((experts, slots), F32)]
    down, put_out, put_grad, scale, mark = call(
        functools.partial(load_body, experts, slots),
        [sds(wd.shape, BF)] + [sds((block, count), BF)] * 2 + [sds((count, 1), F32)],
        [in_hbm(x) for x in (wd, routes[0], gate_values[0])],
        in_specs=[HBM] * 3,
        scratch=[*small, pltpu.SemaphoreType.DMA((3,))],
        mark=True,
    )
    rows = each * n_msg
    n_rows = rows // 2 * SPLIT
    (piece,) = call(
        functools.partial(arrange_body, n_dp, experts, slots, order),
        [sds((rows, half), BF)],
        [got[kinds[m]] for m in order],
        scratch=[pltpu.VMEM((rows, half), F32)],
        extra=rows * half * 8,
        after=[mark],
    )
    own_pieces = [piece] + [send(piece, part_perm(q)) for q in range(2, SPLIT, 2)]
    gate, up, *flipped, last = call(
        flip_body,
        [sds(wg.shape, BF)] * 2 + [sds((hid, half), BF)] * 3,
        (in_hbm(wg), in_hbm(wu), down),
        in_specs=[HBM] * 2 + [VMEM],
        scratch=[pltpu.SemaphoreType.DMA((2,))],
        extra=8 * hid * half,
        mark=True,
    )
    (own_pieces[-1],) = call(hold_body, [sds((rows, half), BF)], [own_pieces[-1]], after=[last])
    sib_pieces = [send(p, part_perm(1)) for p in own_pieces]
    chips = SPLIT // 2
    halves = [(0, chips - 1), tuple(range(1, chips - 1))]
    ordered = [[own_pieces[j] for j in js] + [sib_pieces[j] for j in js] for js in halves]
    mark, parts, recv = (), [], []
    for i, pieces in enumerate(ordered):
        n = len(pieces) * rows // 2
        part, part_sent, *mark = call(
            forward_body,
            [sds((n, 3 * hid), F32), sds((n, 3 * hid), BF)],
            (*pieces, gate, up, down),
            extra=2 * n * half * 2 + n * hid * 4,
            after=mark,
            mark=i == 0,
        )
        parts.append(part)
        recv.append([send(part_sent, batch_perm(dx)) for dx in range(1, n_dp)])
    lefts, sums, mark = [], {}, ()
    for i, js in enumerate(halves):
        n = parts[i].shape[0]
        rows_h, rows_a, rows_b, own, sib, *mark = call(
            functools.partial(backward_body, 2 * len(js), n_dp - 1),
            [sds((n, hid), BF)] * 3 + [sds((n, half), BF)] * 2,
            (parts[i], *recv[i], *flipped),
            extra=n * half * 12,
            after=mark,
            mark=i == 0,
        )
        lefts += [rows_a, rows_b, rows_h]
        got = call(
            pair_sum_body, [sds((rows, half), BF)] * len(js), (own, send(sib, part_perm(1)))
        )
        sums.update(zip(js, got))
    back = [sums[0]] + [send(sums[j], part_perm(2 * j)) for js in halves for j in js if j]
    *grads, mark = call(
        grads_body,
        [sds((1, half, hid), BF)] * 3,
        (*ordered[0], *ordered[1], *lefts),
        out_specs=[HBM] * 3,
        scratch=[pltpu.VMEM((n_rows, half), BF)] * 2
        + [
            pltpu.VMEM((n_rows, hid), BF),
            pltpu.VMEM((3, half, hid), BF),
            pltpu.SemaphoreType.DMA((3,)),
        ],
        extra=n_rows * half * 8 + half * hid * 12,
        mark=True,
        cost=pl.CostEstimate(
            flops=6 * n_rows * half * hid, bytes_accessed=6 * half * hid, transcendentals=0
        ),
    )
    msgs = call(
        functools.partial(return_body, n_dp, experts, slots, len(back), order),
        [sds((each, half), BF)] * n_msg,
        back,
        extra=rows * half * 8,
        after=[mark],
    )
    got = {kinds[m]: msg for m, msg in zip(order, msgs)}
    for kind in kinds[1:]:
        got[kind] = send(got[kind], home_perm(*kind, -1))
    parts = 2
    layer_out, token_grad = call(
        functools.partial(home_body, n_dp, experts, order, parts),
        [sds((block, width), BF)] * 2,
        (put_out, put_grad, scale, *[got[kinds[m]] for m in order]),
        out_specs=[HBM] * 2,
        scratch=[pltpu.VMEM((n_dp, block, half), BF)] * 2
        + [pltpu.VMEM((count, half), F32), pltpu.SemaphoreType.DMA((2 * n_dp * parts,))],
        extra=block * half * 16 + count * half * 4,
    )
    return layer_out, token_grad, *grads


def solution(mesh):
    rows = P(AXES, None)
    slots = P(AXES, None, None)
    weights = P("expert", "dp", None)
    return jax.shard_map(
        functools.partial(shards, mesh.shape["dp"], mesh.shape["expert"]),
        mesh=mesh,
        in_specs=(rows, slots, slots, weights, weights, weights, rows),
        out_specs=(rows, rows, weights, weights, weights),
        check_vma=False,
    )
```

```python
import functools
import math

import jax
import jax.numpy as jnp
from jax import lax
from jax.experimental import pallas as pl
from jax.experimental.pallas import tpu as pltpu
from jax.sharding import PartitionSpec as P

SPLIT = 8
BF = jnp.bfloat16
F32 = jnp.float32
AXES = ("dp", "expert")
TN = (((0,), (0,)), ((), ()))
ANY = pl.BlockSpec(memory_space=pl.ANY)
HBM = pl.BlockSpec(memory_space=pltpu.HBM)
VMEM = pl.BlockSpec(memory_space=pltpu.VMEM)


def mm(a, b, dims=None):
    if dims is None:
        return jnp.dot(a, b, preferred_element_type=F32)
    return lax.dot_general(a, b, dims, preferred_element_type=F32)


def in_hbm(x):
    return pltpu.with_memory_space_constraint(x, pltpu.HBM)


def size(x):
    return math.prod(x.shape) * jnp.dtype(x.dtype).itemsize


def call(
    body,
    out_shape,
    args,
    in_specs=None,
    out_specs=None,
    scratch=(),
    extra=0,
    after=(),
    mark=False,
    cost=None,
):
    n_in, n_out = len(args), len(out_shape)
    used = sum(map(size, args)) + sum(map(size, out_shape)) + extra
    in_specs = in_specs or [VMEM] * n_in
    out_specs = out_specs or [VMEM] * n_out

    def whole(*refs):
        ins, rest = refs[:n_in], refs[n_in + len(after) :]
        outs, rest = rest[:n_out], rest[n_out:]
        if mark:
            rest[0][...] = jnp.zeros_like(rest[0])
            rest = rest[1:]
        body(*ins, *outs, *rest)

    return pl.pallas_call(
        whole,
        out_shape=[*out_shape, *[jax.ShapeDtypeStruct((8, 128), F32)] * mark],
        in_specs=[*in_specs, *[ANY] * len(after)],
        out_specs=[*out_specs, *[VMEM] * mark],
        scratch_shapes=list(scratch),
        compiler_params=pltpu.CompilerParams(vmem_limit_bytes=min(2 * used + (4 << 20), 56 << 20)),
        cost_estimate=cost,
    )(*args, *after)


def slot_values(read, count, slots, expert, experts, axis):
    shape = (count, 1) if axis == 0 else (1, count)
    place = lax.broadcasted_iota(jnp.int32, shape, axis)
    value = None
    for k in range(experts):
        e = lax.rem(expert + k, experts)
        for j in range(2 * slots):
            here = read(e, j % slots)
            if value is None:
                value = jnp.full(shape, here)
            else:
                value = jnp.where(place == k * 2 * slots + j, here, value)
    return value


def own_expert(experts):
    return lax.div(lax.axis_index("expert"), SPLIT)


def gather_body(n_dp, experts, slots, routes_in, gates_in, tokens, cot, *refs):
    *outs, both, routes, gates, sems = refs
    batch = lax.axis_index("dp")
    expert = own_expert(experts)
    count = 2 * slots * experts
    block = tokens.shape[0]
    half = tokens.shape[1] // n_dp
    moves = [(routes_in, routes), (gates_in, gates)]
    for dx in range(n_dp):
        at = pl.ds(pl.multiple_of(lax.rem(batch + dx, n_dp) * half, 128), half)
        for i, src in enumerate((tokens, cot)):
            moves.append((src.at[:, at], both.at[dx, pl.ds(i * block, block)]))
    copies = [pltpu.make_async_copy(*move, sems.at[i]) for i, move in enumerate(moves)]
    for copy in copies:
        copy.start()
    for copy in copies[:2]:
        copy.wait()
    pos = slot_values(lambda e, s: routes[e, s], count, slots, expert, experts, 0)
    gate = slot_values(lambda e, s: gates[e, s], count, slots, expert, experts, 0)
    is_token = lax.rem(lax.broadcasted_iota(jnp.int32, (count, 1), 0), 2 * slots) < slots
    scale = jnp.where(is_token, 1.0, gate)
    row = jnp.where(is_token, pos, pos + block)
    hit = lax.broadcasted_iota(jnp.int32, (count, 2 * block), 1) == row
    pick = jnp.where(hit, 1.0, 0.0).astype(BF)
    for dx in range(n_dp):
        for copy in copies[2 + 2 * dx : 4 + 2 * dx]:
            copy.wait()
        rows = (mm(pick, both[dx]) * scale).astype(BF)
        for k in range(experts):
            outs[dx * experts + k][...] = rows[k * 2 * slots : (k + 1) * 2 * slots]


def row_map(n_dp, ks, slots, batch, to_block):
    each = 2 * slots
    total = each * n_dp * ks
    r = lax.broadcasted_iota(jnp.int32, (total, 1), 0)
    if to_block:
        kind, rest = lax.div(r, total // 2), lax.rem(r, total // 2)
        b, rest = lax.div(rest, ks * slots), lax.rem(rest, ks * slots)
        k, s = lax.div(rest, slots), lax.rem(rest, slots)
        dx = lax.rem(batch - b + n_dp, n_dp)
        source = (dx * ks + k) * each + kind * slots + s
    else:
        m, j = lax.div(r, each), lax.rem(r, each)
        dx, k = lax.div(m, ks), lax.rem(m, ks)
        kind, s = lax.div(j, slots), lax.rem(j, slots)
        b = lax.rem(batch - dx + n_dp, n_dp)
        source = kind * (total // 2) + (b * ks + k) * slots + s
    pick = lax.broadcasted_iota(jnp.int32, (total, total), 1) == source
    return jnp.where(pick, 1.0, 0.0).astype(BF)


def arrange_body(n_dp, experts, slots, order, *refs):
    *msgs, out, wide = refs
    each = 2 * slots
    for m, msg in zip(order, msgs):
        wide[m * each : (m + 1) * each, :] = msg[...].astype(F32)
    pick = row_map(n_dp, experts, slots, lax.axis_index("dp"), True)
    out[...] = mm(pick, wide[...].astype(BF)).astype(BF)


def prepare_body(experts, slots, routes_in, gates_in, put_out, put_grad, scale, routes, gates, sems):
    moves = ((routes_in, routes), (gates_in, gates))
    copies = [pltpu.make_async_copy(*move, sems.at[i]) for i, move in enumerate(moves)]
    for copy in copies:
        copy.start()
    for copy in copies:
        copy.wait()
    expert = own_expert(experts)
    each = 2 * slots
    count = each * experts
    block = put_out.shape[0]
    pos = slot_values(lambda e, s: routes[e, s], count, slots, expert, experts, 1)
    gate = slot_values(lambda e, s: gates[e, s], count, slots, expert, experts, 0)
    is_out = lax.rem(lax.broadcasted_iota(jnp.int32, (count, 1), 0), each) < slots
    is_out_lane = lax.rem(lax.broadcasted_iota(jnp.int32, (1, count), 1), each) < slots
    scale[...] = jnp.where(is_out, gate, 1.0)
    hit = lax.broadcasted_iota(jnp.int32, (block, count), 0) == pos
    put_out[...] = jnp.where(hit & is_out_lane, 1.0, 0.0).astype(BF)
    put_grad[...] = jnp.where(hit & ~is_out_lane, 1.0, 0.0).astype(BF)


def forward_body(*refs):
    *pieces, wg, wu, wd, part, part_sent = refs
    n = pieces[0].shape[0] // 2
    hid = wg.shape[2]
    xs = jnp.concatenate([piece[:n, :] for piece in pieces], axis=0)
    ys = jnp.concatenate([piece[n:, :] for piece in pieces], axis=0)
    for i, (rows, w) in enumerate(((xs, wg), (xs, wu), (ys, wd))):
        got = mm(rows, w[0])
        part[:, i * hid : (i + 1) * hid] = got
        part_sent[:, i * hid : (i + 1) * hid] = got.astype(BF)


def hold_body(src, dst):
    dst[...] = src[...]


def flip_body(*refs):
    srcs, dsts, flipped, sems = refs[:3], refs[3:6], refs[6:9], refs[9]
    copies = [
        pltpu.make_async_copy(src, dst, sems.at[i]) for i, (src, dst) in enumerate(zip(srcs, dsts))
    ]
    for copy in copies:
        copy.start()
    for copy, src, dst in zip(copies, dsts, flipped):
        copy.wait()
        dst[...] = src[0].T


def backward_body(n_pieces, n_recv, *refs):
    part, *rest = refs
    recv, rest = rest[:n_recv], rest[n_recv:]
    wg, wu, wd, rows_h, rows_a, rows_b, own, sib = rest
    hid = wg.shape[0]
    total = part[...]
    for other in recv:
        total = total + other[...].astype(F32)
    g, u, q = total[:, :hid], total[:, hid : 2 * hid], total[:, 2 * hid :]
    sig = jax.nn.sigmoid(g)
    h = (g * sig * u).astype(BF)
    a = (q * u * sig * (1.0 + g * (1.0 - sig))).astype(BF)
    b = (q * g * sig).astype(BF)
    rows_h[...] = h
    rows_a[...] = a
    rows_b[...] = b
    p = mm(h, wd[...]).astype(BF)
    e = (mm(a, wg[...]) + mm(b, wu[...])).astype(BF)
    n = part.shape[0] // n_pieces
    for i in range(n_pieces):
        out, at = (own, i) if 2 * i < n_pieces else (sib, i - n_pieces // 2)
        out[2 * at * n : (2 * at + 1) * n, :] = p[i * n : (i + 1) * n]
        out[(2 * at + 1) * n : (2 * at + 2) * n, :] = e[i * n : (i + 1) * n]


def pair_sum_body(own, got, *outs):
    n = own.shape[0] // len(outs)
    for j, out in enumerate(outs):
        at = slice(j * n, (j + 1) * n)
        out[...] = (own[at, :].astype(F32) + got[at, :].astype(F32)).astype(BF)


def return_body(n_dp, ks, slots, n_in, order, *refs):
    ins, outs = refs[:n_in], refs[n_in:]
    each = 2 * slots
    value = ins[0][...].astype(F32)
    for other in ins[1:]:
        value = value + other[...].astype(F32)
    pick = row_map(n_dp, ks, slots, lax.axis_index("dp"), False)
    rows = mm(pick, value.astype(BF)).astype(BF)
    for m, out in zip(order, outs):
        out[...] = rows[m * each : (m + 1) * each]


def home_body(n_dp, experts, order, parts, put_out, put_grad, scale, *refs):
    msgs, outs, (layer_half, grad_half, wide, sems) = refs[:-6], refs[-6:-4], refs[-4:]
    msgs = dict(zip(order, msgs))
    batch = lax.axis_index("dp")
    each = msgs[0].shape[0]
    half = layer_half.shape[2]
    step = half // parts
    put_out, put_grad, scale = put_out[...], put_grad[...], scale[...]
    put_both = jnp.concatenate([put_out, put_out], axis=1)
    copies = []
    for dx in range(n_dp):
        for k in range(experts):
            wide[k * each : (k + 1) * each, :] = msgs[dx * experts + k][...].astype(F32)
        first = lax.rem(batch + dx, n_dp) * half
        for c in range(parts):
            at = slice(c * step, (c + 1) * step)
            value = wide[:, at] * scale
            high = value.astype(BF)
            low = (value - high.astype(F32)).astype(BF)
            grad_half[dx, :, at] = mm(put_grad, high).astype(BF)
            layer_half[dx, :, at] = mm(put_both, jnp.concatenate([high, low], axis=0)).astype(BF)
            to = pl.ds(pl.multiple_of(first + c * step, 128), step)
            for src, dst in ((grad_half, outs[1]), (layer_half, outs[0])):
                copy = pltpu.make_async_copy(
                    src.at[dx, :, pl.ds(c * step, step)], dst.at[:, to], sems.at[len(copies)]
                )
                copy.start()
                copies.append(copy)
    for copy in copies:
        copy.wait()


def grads_body(*refs):
    pieces, lefts, (*outs, xs, ys, w, held, sems) = (
        refs[:SPLIT],
        refs[SPLIT : SPLIT + 6],
        refs[SPLIT + 6 :],
    )
    n = pieces[0].shape[0] // 2
    for i, piece in enumerate(pieces):
        xs[i * n : (i + 1) * n, :] = piece[:n, :]
        ys[i * n : (i + 1) * n, :] = piece[n:, :]
    copies = []
    for i, rows in enumerate((xs, xs, ys)):
        for j in range(2):
            left = lefts[3 * j + i]
            w[j * left.shape[0] : (j + 1) * left.shape[0], :] = left[...]
        held[i] = mm(rows[...], w[...], TN).astype(BF)
        copies.append(pltpu.make_async_copy(held.at[i], outs[i].at[0], sems.at[i]))
        copies[-1].start()
    for copy in copies:
        copy.wait()


def shards(n_dp, n_exp, tokens, routes, gate_values, wg, wu, wd, cot):
    block, width = tokens.shape
    experts = routes.shape[1]
    slots = routes.shape[2]
    hid = wg.shape[2]
    half = width // n_dp
    each = 2 * slots
    n_msg = n_dp * experts
    sds = jax.ShapeDtypeStruct

    def home_perm(dx, k, sign):
        return [
            (
                d * n_exp + i,
                (d + sign * dx) % n_dp * n_exp + (i // SPLIT + sign * k) % experts * SPLIT + i % SPLIT,
            )
            for d in range(n_dp)
            for i in range(n_exp)
        ]

    def part_perm(q):
        return [(d * n_exp + i, d * n_exp + (i ^ q)) for d in range(n_dp) for i in range(n_exp)]

    def batch_perm(dx):
        return [
            (d * n_exp + i, (d + dx) % n_dp * n_exp + i) for d in range(n_dp) for i in range(n_exp)
        ]

    def send(x, perm):
        return lax.ppermute(x, AXES, perm)

    kinds = [(dx, k) for dx in range(n_dp) for k in range(experts)]
    order = sorted(range(n_msg), key=lambda m: (kinds[m][1] == 0, kinds[m][0] == 0, m))
    small = [sds((each, half), BF)] * n_msg
    msgs = call(
        functools.partial(gather_body, n_dp, experts, slots),
        small,
        [in_hbm(x) for x in (routes[0], gate_values[0], tokens, cot)],
        in_specs=[HBM] * 4,
        scratch=[
            pltpu.VMEM((n_dp, 2 * block, half), BF),
            pltpu.SMEM((experts, slots), jnp.int32),
            pltpu.SMEM((experts, slots), F32),
            pltpu.SemaphoreType.DMA((2 + 2 * n_dp,)),
        ],
    )
    got = dict(zip(kinds, msgs))
    for kind in kinds[1:]:
        got[kind] = send(got[kind], home_perm(*kind, 1))
    count = each * experts
    small = [pltpu.SMEM((experts, slots), jnp.int32), pltpu.SMEM((experts, slots), F32)]
    put_out, put_grad, scale, mark = call(
        functools.partial(prepare_body, experts, slots),
        [sds((block, count), BF)] * 2 + [sds((count, 1), F32)],
        [in_hbm(x) for x in (routes[0], gate_values[0])],
        in_specs=[HBM] * 2,
        scratch=[*small, pltpu.SemaphoreType.DMA((2,))],
        mark=True,
    )
    rows = each * n_msg
    n_rows = rows // 2 * SPLIT
    (piece,) = call(
        functools.partial(arrange_body, n_dp, experts, slots, order),
        [sds((rows, half), BF)],
        [got[kinds[m]] for m in order],
        scratch=[pltpu.VMEM((rows, half), F32)],
        extra=rows * half * 8,
        after=[mark],
    )
    own_pieces = [piece] + [send(piece, part_perm(q)) for q in range(2, SPLIT, 2)]
    gate, up, down, *flipped, last = call(
        flip_body,
        [sds(wg.shape, BF)] * 3 + [sds((hid, half), BF)] * 3,
        [in_hbm(x) for x in (wg, wu, wd)],
        in_specs=[HBM] * 3,
        scratch=[pltpu.SemaphoreType.DMA((3,))],
        extra=8 * hid * half,
        mark=True,
    )
    (own_pieces[-1],) = call(hold_body, [sds((rows, half), BF)], [own_pieces[-1]], after=[last])
    sib_pieces = [send(p, part_perm(1)) for p in own_pieces]
    chips = SPLIT // 2
    halves = [(0, chips - 1), tuple(range(1, chips - 1))]
    ordered = [[own_pieces[j] for j in js] + [sib_pieces[j] for j in js] for js in halves]
    mark, parts, recv = (), [], []
    for i, pieces in enumerate(ordered):
        n = len(pieces) * rows // 2
        part, part_sent, *mark = call(
            forward_body,
            [sds((n, 3 * hid), F32), sds((n, 3 * hid), BF)],
            (*pieces, gate, up, down),
            extra=2 * n * half * 2 + n * hid * 4,
            after=mark,
            mark=i == 0,
        )
        parts.append(part)
        recv.append([send(part_sent, batch_perm(dx)) for dx in range(1, n_dp)])
    lefts, sums, mark = [], {}, ()
    for i, js in enumerate(halves):
        n = parts[i].shape[0]
        rows_h, rows_a, rows_b, own, sib, *mark = call(
            functools.partial(backward_body, 2 * len(js), n_dp - 1),
            [sds((n, hid), BF)] * 3 + [sds((n, half), BF)] * 2,
            (parts[i], *recv[i], *flipped),
            extra=n * half * 12,
            after=mark,
            mark=i == 0,
        )
        lefts += [rows_a, rows_b, rows_h]
        got = call(
            pair_sum_body, [sds((rows, half), BF)] * len(js), (own, send(sib, part_perm(1)))
        )
        sums.update(zip(js, got))
    back = [sums[0]] + [send(sums[j], part_perm(2 * j)) for js in halves for j in js if j]
    *grads, mark = call(
        grads_body,
        [sds((1, half, hid), BF)] * 3,
        (*ordered[0], *ordered[1], *lefts),
        out_specs=[HBM] * 3,
        scratch=[pltpu.VMEM((n_rows, half), BF)] * 2
        + [
            pltpu.VMEM((n_rows, hid), BF),
            pltpu.VMEM((3, half, hid), BF),
            pltpu.SemaphoreType.DMA((3,)),
        ],
        extra=n_rows * half * 8 + half * hid * 12,
        mark=True,
        cost=pl.CostEstimate(
            flops=6 * n_rows * half * hid, bytes_accessed=6 * half * hid, transcendentals=0
        ),
    )
    msgs = call(
        functools.partial(return_body, n_dp, experts, slots, len(back), order),
        [sds((each, half), BF)] * n_msg,
        back,
        extra=rows * half * 8,
        after=[mark],
    )
    got = {kinds[m]: msg for m, msg in zip(order, msgs)}
    for kind in kinds[1:]:
        got[kind] = send(got[kind], home_perm(*kind, -1))
    parts = 2
    layer_out, token_grad = call(
        functools.partial(home_body, n_dp, experts, order, parts),
        [sds((block, width), BF)] * 2,
        (put_out, put_grad, scale, *[got[kinds[m]] for m in order]),
        out_specs=[HBM] * 2,
        scratch=[pltpu.VMEM((n_dp, block, half), BF)] * 2
        + [pltpu.VMEM((count, half), F32), pltpu.SemaphoreType.DMA((2 * n_dp * parts,))],
        extra=block * half * 16 + count * half * 4,
    )
    return layer_out, token_grad, *grads


def solution(mesh):
    rows = P(AXES, None)
    slots = P(AXES, None, None)
    weights = P("expert", "dp", None)
    return jax.shard_map(
        functools.partial(shards, mesh.shape["dp"], mesh.shape["expert"]),
        mesh=mesh,
        in_specs=(rows, slots, slots, weights, weights, weights, rows),
        out_specs=(rows, rows, weights, weights, weights),
        check_vma=False,
    )
```

```python
import functools
import math

import jax
import jax.numpy as jnp
from jax import lax
from jax.experimental import pallas as pl
from jax.experimental.pallas import tpu as pltpu
from jax.sharding import PartitionSpec as P

SPLIT = 8
BF = jnp.bfloat16
F32 = jnp.float32
AXES = ("dp", "expert")
TN = (((0,), (0,)), ((), ()))
ANY = pl.BlockSpec(memory_space=pl.ANY)
HBM = pl.BlockSpec(memory_space=pltpu.HBM)
VMEM = pl.BlockSpec(memory_space=pltpu.VMEM)


def mm(a, b, dims=None):
    if dims is None:
        return jnp.dot(a, b, preferred_element_type=F32)
    return lax.dot_general(a, b, dims, preferred_element_type=F32)


def in_hbm(x):
    return pltpu.with_memory_space_constraint(x, pltpu.HBM)


def size(x):
    return math.prod(x.shape) * jnp.dtype(x.dtype).itemsize


def call(
    body,
    out_shape,
    args,
    in_specs=None,
    out_specs=None,
    scratch=(),
    extra=0,
    after=(),
    mark=False,
    cost=None,
):
    n_in, n_out = len(args), len(out_shape)
    used = sum(map(size, args)) + sum(map(size, out_shape)) + extra
    in_specs = in_specs or [VMEM] * n_in
    out_specs = out_specs or [VMEM] * n_out

    def whole(*refs):
        ins, rest = refs[:n_in], refs[n_in + len(after) :]
        outs, rest = rest[:n_out], rest[n_out:]
        if mark:
            rest[0][...] = jnp.zeros_like(rest[0])
            rest = rest[1:]
        body(*ins, *outs, *rest)

    return pl.pallas_call(
        whole,
        out_shape=[*out_shape, *[jax.ShapeDtypeStruct((8, 128), F32)] * mark],
        in_specs=[*in_specs, *[ANY] * len(after)],
        out_specs=[*out_specs, *[VMEM] * mark],
        scratch_shapes=list(scratch),
        compiler_params=pltpu.CompilerParams(vmem_limit_bytes=min(2 * used + (4 << 20), 56 << 20)),
        cost_estimate=cost,
    )(*args, *after)


def slot_values(read, count, slots, expert, experts, axis):
    shape = (count, 1) if axis == 0 else (1, count)
    place = lax.broadcasted_iota(jnp.int32, shape, axis)
    value = None
    for k in range(experts):
        e = lax.rem(expert + k, experts)
        for j in range(2 * slots):
            here = read(e, j % slots)
            if value is None:
                value = jnp.full(shape, here)
            else:
                value = jnp.where(place == k * 2 * slots + j, here, value)
    return value


def own_expert(experts):
    return lax.div(lax.axis_index("expert"), SPLIT)


def gather_body(n_dp, experts, slots, routes_in, gates_in, tokens, cot, *refs):
    *outs, both, routes, gates, sems = refs
    batch = lax.axis_index("dp")
    expert = own_expert(experts)
    count = 2 * slots * experts
    block = tokens.shape[0]
    half = tokens.shape[1] // n_dp
    moves = [(routes_in, routes), (gates_in, gates)]
    for dx in range(n_dp):
        at = pl.ds(pl.multiple_of(lax.rem(batch + dx, n_dp) * half, 128), half)
        for i, src in enumerate((tokens, cot)):
            moves.append((src.at[:, at], both.at[dx, pl.ds(i * block, block)]))
    copies = [pltpu.make_async_copy(*move, sems.at[i]) for i, move in enumerate(moves)]
    for copy in copies[2:] + copies[:2]:
        copy.start()
    for copy in copies[:2]:
        copy.wait()
    pos = slot_values(lambda e, s: routes[e, s], count, slots, expert, experts, 0)
    gate = slot_values(lambda e, s: gates[e, s], count, slots, expert, experts, 0)
    is_token = lax.rem(lax.broadcasted_iota(jnp.int32, (count, 1), 0), 2 * slots) < slots
    scale = jnp.where(is_token, 1.0, gate)
    row = jnp.where(is_token, pos, pos + block)
    hit = lax.broadcasted_iota(jnp.int32, (count, 2 * block), 1) == row
    pick = jnp.where(hit, 1.0, 0.0).astype(BF)
    for dx in range(n_dp):
        for copy in copies[2 + 2 * dx : 4 + 2 * dx]:
            copy.wait()
        rows = (mm(pick, both[dx]) * scale).astype(BF)
        for k in range(experts):
            outs[dx * experts + k][...] = rows[k * 2 * slots : (k + 1) * 2 * slots]


def row_map(n_dp, ks, slots, batch, to_block):
    each = 2 * slots
    total = each * n_dp * ks
    r = lax.broadcasted_iota(jnp.int32, (total, 1), 0)
    if to_block:
        kind, rest = lax.div(r, total // 2), lax.rem(r, total // 2)
        b, rest = lax.div(rest, ks * slots), lax.rem(rest, ks * slots)
        k, s = lax.div(rest, slots), lax.rem(rest, slots)
        dx = lax.rem(batch - b + n_dp, n_dp)
        source = (dx * ks + k) * each + kind * slots + s
    else:
        m, j = lax.div(r, each), lax.rem(r, each)
        dx, k = lax.div(m, ks), lax.rem(m, ks)
        kind, s = lax.div(j, slots), lax.rem(j, slots)
        b = lax.rem(batch - dx + n_dp, n_dp)
        source = kind * (total // 2) + (b * ks + k) * slots + s
    pick = lax.broadcasted_iota(jnp.int32, (total, total), 1) == source
    return jnp.where(pick, 1.0, 0.0).astype(BF)


def arrange_body(n_dp, experts, slots, order, *refs):
    *msgs, out, wide = refs
    each = 2 * slots
    for m, msg in zip(order, msgs):
        wide[m * each : (m + 1) * each, :] = msg[...].astype(F32)
    pick = row_map(n_dp, experts, slots, lax.axis_index("dp"), True)
    out[...] = mm(pick, wide[...].astype(BF)).astype(BF)


def prepare_body(experts, slots, routes_in, gates_in, put_out, put_grad, scale, routes, gates, sems):
    moves = ((routes_in, routes), (gates_in, gates))
    copies = [pltpu.make_async_copy(*move, sems.at[i]) for i, move in enumerate(moves)]
    for copy in copies:
        copy.start()
    for copy in copies:
        copy.wait()
    expert = own_expert(experts)
    each = 2 * slots
    count = each * experts
    block = put_out.shape[0]
    pos = slot_values(lambda e, s: routes[e, s], count, slots, expert, experts, 1)
    gate = slot_values(lambda e, s: gates[e, s], count, slots, expert, experts, 0)
    is_out = lax.rem(lax.broadcasted_iota(jnp.int32, (count, 1), 0), each) < slots
    is_out_lane = lax.rem(lax.broadcasted_iota(jnp.int32, (1, count), 1), each) < slots
    scale[...] = jnp.where(is_out, gate, 1.0)
    hit = lax.broadcasted_iota(jnp.int32, (block, count), 0) == pos
    put_out[...] = jnp.where(hit & is_out_lane, 1.0, 0.0).astype(BF)
    put_grad[...] = jnp.where(hit & ~is_out_lane, 1.0, 0.0).astype(BF)


def forward_body(*refs):
    *pieces, wg, wu, wd, part, part_sent = refs
    n = pieces[0].shape[0] // 2
    hid = wg.shape[2]
    xs = jnp.concatenate([piece[:n, :] for piece in pieces], axis=0)
    ys = jnp.concatenate([piece[n:, :] for piece in pieces], axis=0)
    for i, (rows, w) in enumerate(((xs, wg), (xs, wu), (ys, wd))):
        got = mm(rows, w[0])
        part[:, i * hid : (i + 1) * hid] = got
        part_sent[:, i * hid : (i + 1) * hid] = got.astype(BF)


def hold_body(src, dst):
    dst[...] = src[...]


def flip_body(*refs):
    srcs, dsts, flipped, sems = refs[:3], refs[3:6], refs[6:9], refs[9]
    copies = [
        pltpu.make_async_copy(src, dst, sems.at[i]) for i, (src, dst) in enumerate(zip(srcs, dsts))
    ]
    for copy in copies:
        copy.start()
    for copy, src, dst in zip(copies, dsts, flipped):
        copy.wait()
        dst[...] = src[0].T


def backward_body(n_pieces, n_recv, *refs):
    part, *rest = refs
    recv, rest = rest[:n_recv], rest[n_recv:]
    wg, wu, wd, rows_h, rows_a, rows_b, own, sib = rest
    hid = wg.shape[0]
    total = part[...]
    for other in recv:
        total = total + other[...].astype(F32)
    g, u, q = total[:, :hid], total[:, hid : 2 * hid], total[:, 2 * hid :]
    sig = jax.nn.sigmoid(g)
    h = (g * sig * u).astype(BF)
    a = (q * u * sig * (1.0 + g * (1.0 - sig))).astype(BF)
    b = (q * g * sig).astype(BF)
    rows_h[...] = h
    rows_a[...] = a
    rows_b[...] = b
    p = mm(h, wd[...]).astype(BF)
    e = (mm(a, wg[...]) + mm(b, wu[...])).astype(BF)
    n = part.shape[0] // n_pieces
    for i in range(n_pieces):
        out, at = (own, i) if 2 * i < n_pieces else (sib, i - n_pieces // 2)
        out[2 * at * n : (2 * at + 1) * n, :] = p[i * n : (i + 1) * n]
        out[(2 * at + 1) * n : (2 * at + 2) * n, :] = e[i * n : (i + 1) * n]


def pair_sum_body(own, got, *outs):
    n = own.shape[0] // len(outs)
    for j, out in enumerate(outs):
        at = slice(j * n, (j + 1) * n)
        out[...] = (own[at, :].astype(F32) + got[at, :].astype(F32)).astype(BF)


def return_body(n_dp, ks, slots, n_in, order, *refs):
    ins, outs = refs[:n_in], refs[n_in:]
    each = 2 * slots
    value = ins[0][...].astype(F32)
    for other in ins[1:]:
        value = value + other[...].astype(F32)
    pick = row_map(n_dp, ks, slots, lax.axis_index("dp"), False)
    rows = mm(pick, value.astype(BF)).astype(BF)
    for m, out in zip(order, outs):
        out[...] = rows[m * each : (m + 1) * each]


def home_body(n_dp, experts, order, parts, put_out, put_grad, scale, *refs):
    msgs, outs, (layer_half, grad_half, wide, sems) = refs[:-6], refs[-6:-4], refs[-4:]
    msgs = dict(zip(order, msgs))
    batch = lax.axis_index("dp")
    each = msgs[0].shape[0]
    half = layer_half.shape[2]
    step = half // parts
    put_out, put_grad, scale = put_out[...], put_grad[...], scale[...]
    put_both = jnp.concatenate([put_out, put_out], axis=1)
    copies = []
    for dx in range(n_dp):
        for k in range(experts):
            wide[k * each : (k + 1) * each, :] = msgs[dx * experts + k][...].astype(F32)
        first = lax.rem(batch + dx, n_dp) * half
        for c in range(parts):
            at = slice(c * step, (c + 1) * step)
            value = wide[:, at] * scale
            high = value.astype(BF)
            low = (value - high.astype(F32)).astype(BF)
            grad_half[dx, :, at] = mm(put_grad, high).astype(BF)
            layer_half[dx, :, at] = mm(put_both, jnp.concatenate([high, low], axis=0)).astype(BF)
            to = pl.ds(pl.multiple_of(first + c * step, 128), step)
            for src, dst in ((grad_half, outs[1]), (layer_half, outs[0])):
                copy = pltpu.make_async_copy(
                    src.at[dx, :, pl.ds(c * step, step)], dst.at[:, to], sems.at[len(copies)]
                )
                copy.start()
                copies.append(copy)
    for copy in copies:
        copy.wait()


def grads_body(*refs):
    pieces, lefts, (*outs, xs, ys, w, held, sems) = (
        refs[:SPLIT],
        refs[SPLIT : SPLIT + 6],
        refs[SPLIT + 6 :],
    )
    n = pieces[0].shape[0] // 2
    for i, piece in enumerate(pieces):
        xs[i * n : (i + 1) * n, :] = piece[:n, :]
        ys[i * n : (i + 1) * n, :] = piece[n:, :]
    copies = []
    for i, rows in enumerate((xs, xs, ys)):
        for j in range(2):
            left = lefts[3 * j + i]
            w[j * left.shape[0] : (j + 1) * left.shape[0], :] = left[...]
        held[i] = mm(rows[...], w[...], TN).astype(BF)
        copies.append(pltpu.make_async_copy(held.at[i], outs[i].at[0], sems.at[i]))
        copies[-1].start()
    for copy in copies:
        copy.wait()


def shards(n_dp, n_exp, tokens, routes, gate_values, wg, wu, wd, cot):
    block, width = tokens.shape
    experts = routes.shape[1]
    slots = routes.shape[2]
    hid = wg.shape[2]
    half = width // n_dp
    each = 2 * slots
    n_msg = n_dp * experts
    sds = jax.ShapeDtypeStruct

    def home_perm(dx, k, sign):
        return [
            (
                d * n_exp + i,
                (d + sign * dx) % n_dp * n_exp + (i // SPLIT + sign * k) % experts * SPLIT + i % SPLIT,
            )
            for d in range(n_dp)
            for i in range(n_exp)
        ]

    def part_perm(q):
        return [(d * n_exp + i, d * n_exp + (i ^ q)) for d in range(n_dp) for i in range(n_exp)]

    def batch_perm(dx):
        return [
            (d * n_exp + i, (d + dx) % n_dp * n_exp + i) for d in range(n_dp) for i in range(n_exp)
        ]

    def send(x, perm):
        return lax.ppermute(x, AXES, perm)

    kinds = [(dx, k) for dx in range(n_dp) for k in range(experts)]
    order = sorted(range(n_msg), key=lambda m: (kinds[m][1] == 0, kinds[m][0] == 0, m))
    small = [sds((each, half), BF)] * n_msg
    msgs = call(
        functools.partial(gather_body, n_dp, experts, slots),
        small,
        [in_hbm(x) for x in (routes[0], gate_values[0], tokens, cot)],
        in_specs=[HBM] * 4,
        scratch=[
            pltpu.VMEM((n_dp, 2 * block, half), BF),
            pltpu.SMEM((experts, slots), jnp.int32),
            pltpu.SMEM((experts, slots), F32),
            pltpu.SemaphoreType.DMA((2 + 2 * n_dp,)),
        ],
    )
    got = dict(zip(kinds, msgs))
    for kind in kinds[1:]:
        got[kind] = send(got[kind], home_perm(*kind, 1))
    count = each * experts
    small = [pltpu.SMEM((experts, slots), jnp.int32), pltpu.SMEM((experts, slots), F32)]
    put_out, put_grad, scale, mark = call(
        functools.partial(prepare_body, experts, slots),
        [sds((block, count), BF)] * 2 + [sds((count, 1), F32)],
        [in_hbm(x) for x in (routes[0], gate_values[0])],
        in_specs=[HBM] * 2,
        scratch=[*small, pltpu.SemaphoreType.DMA((2,))],
        mark=True,
    )
    rows = each * n_msg
    n_rows = rows // 2 * SPLIT
    (piece,) = call(
        functools.partial(arrange_body, n_dp, experts, slots, order),
        [sds((rows, half), BF)],
        [got[kinds[m]] for m in order],
        scratch=[pltpu.VMEM((rows, half), F32)],
        extra=rows * half * 8,
        after=[mark],
    )
    own_pieces = [piece] + [send(piece, part_perm(q)) for q in range(2, SPLIT, 2)]
    gate, up, down, *flipped, last = call(
        flip_body,
        [sds(wg.shape, BF)] * 3 + [sds((hid, half), BF)] * 3,
        [in_hbm(x) for x in (wg, wu, wd)],
        in_specs=[HBM] * 3,
        scratch=[pltpu.SemaphoreType.DMA((3,))],
        extra=8 * hid * half,
        mark=True,
    )
    (own_pieces[-1],) = call(hold_body, [sds((rows, half), BF)], [own_pieces[-1]], after=[last])
    sib_pieces = [send(p, part_perm(1)) for p in own_pieces]
    chips = SPLIT // 2
    halves = [(0, chips - 1), tuple(range(1, chips - 1))]
    ordered = [[own_pieces[j] for j in js] + [sib_pieces[j] for j in js] for js in halves]
    parts, recv = [], []
    for pieces in ordered:
        n = len(pieces) * rows // 2
        part, part_sent = call(
            forward_body,
            [sds((n, 3 * hid), F32), sds((n, 3 * hid), BF)],
            (*pieces, gate, up, down),
            extra=2 * n * half * 2 + n * hid * 4,
        )
        parts.append(part)
        recv.append([send(part_sent, batch_perm(dx)) for dx in range(1, n_dp)])
    lefts, sums, mark = [], {}, ()
    for i, js in enumerate(halves):
        n = parts[i].shape[0]
        rows_h, rows_a, rows_b, own, sib, *mark = call(
            functools.partial(backward_body, 2 * len(js), n_dp - 1),
            [sds((n, hid), BF)] * 3 + [sds((n, half), BF)] * 2,
            (parts[i], *recv[i], *flipped),
            extra=n * half * 12,
            after=mark,
            mark=i == 0,
        )
        lefts += [rows_a, rows_b, rows_h]
        got = call(
            pair_sum_body, [sds((rows, half), BF)] * len(js), (own, send(sib, part_perm(1)))
        )
        sums.update(zip(js, got))
    back = [sums[0]] + [send(sums[j], part_perm(2 * j)) for js in halves for j in js if j]
    *grads, mark = call(
        grads_body,
        [sds((1, half, hid), BF)] * 3,
        (*ordered[0], *ordered[1], *lefts),
        out_specs=[HBM] * 3,
        scratch=[pltpu.VMEM((n_rows, half), BF)] * 2
        + [
            pltpu.VMEM((n_rows, hid), BF),
            pltpu.VMEM((3, half, hid), BF),
            pltpu.SemaphoreType.DMA((3,)),
        ],
        extra=n_rows * half * 8 + half * hid * 12,
        mark=True,
        cost=pl.CostEstimate(
            flops=6 * n_rows * half * hid, bytes_accessed=6 * half * hid, transcendentals=0
        ),
    )
    msgs = call(
        functools.partial(return_body, n_dp, experts, slots, len(back), order),
        [sds((each, half), BF)] * n_msg,
        back,
        extra=rows * half * 8,
        after=[mark],
    )
    got = {kinds[m]: msg for m, msg in zip(order, msgs)}
    for kind in kinds[1:]:
        got[kind] = send(got[kind], home_perm(*kind, -1))
    parts = 2
    layer_out, token_grad = call(
        functools.partial(home_body, n_dp, experts, order, parts),
        [sds((block, width), BF)] * 2,
        (put_out, put_grad, scale, *[got[kinds[m]] for m in order]),
        out_specs=[HBM] * 2,
        scratch=[pltpu.VMEM((n_dp, block, half), BF)] * 2
        + [pltpu.VMEM((count, half), F32), pltpu.SemaphoreType.DMA((2 * n_dp * parts,))],
        extra=block * half * 16 + count * half * 4,
    )
    return layer_out, token_grad, *grads


def solution(mesh):
    rows = P(AXES, None)
    slots = P(AXES, None, None)
    weights = P("expert", "dp", None)
    return jax.shard_map(
        functools.partial(shards, mesh.shape["dp"], mesh.shape["expert"]),
        mesh=mesh,
        in_specs=(rows, slots, slots, weights, weights, weights, rows),
        out_specs=(rows, rows, weights, weights, weights),
        check_vma=False,
    )
```
